32 devices in a mesh: group: 2 (over y), expert: 8 (over z, x), tensor: 2 (over core).
Axes of the slice: x: 2, y: 2, z: 4, core: 2. Of those that a mesh axis runs over, the one named last changes fastest.
Arguments:
- tokens: bfloat16 [1024, 3584], P(('group', 'expert'), 'tensor'), parts along dimension 0, may hold values from -6 to 6
- expert_ids: int32 [1024, 2], P(('group', 'expert')), parts along dimension 0, may hold values from 0 to 7, all different within a row; in each aligned block of 64 rows (0 to 63, 64 to 127, ...) at most 20 rows name the same one
- gate_weights: float32 [1024, 2], P(('group', 'expert')), parts along dimension 0, may hold values from 0.1 to 0.6
- w_gate: bfloat16 [3584, 16384], P('tensor', 'expert'), may hold values from -0.09375 to 0.09375
- w_up: bfloat16 [3584, 16384], P('tensor', 'expert'), may hold values from -0.09375 to 0.09375
- w_down: bfloat16 [16384, 3584], P('expert', 'tensor'), may hold values from -0.125 to 0.125
Outputs:
- combined: bfloat16 [1024, 3584], P(('group', 'expert'), 'tensor'), parts along dimension 0
The draws below stay inside these ranges and needn't reach their ends.
There are 2 independent parts, one for each index of `group`. The reference program is written for one: setup_inputs(seed, part) draws one part's arguments, and reference() takes and returns one part's arrays. A program takes and returns all parts, laid end to end along the dimension named above; an argument that names none is the same for every part. Nothing has to cross between parts.
Inputs may be any that keep to these rules, and one draw needn't show every extreme that they name: `expert_ids`: each row names 2 different experts. In each aligned block of 64 rows, no expert is named by more than 20 rows; in some blocks an expert is named by exactly 20 rows.
All inputs are finite; a program needn't handle non-finite values.
Results may differ from the reference program's by a relative error of at most 0.015.
Values may be sent and summed in bfloat16 or wider, within the bound.
No kernel may reach another device: no remote copies, remote signals or barrier semaphores. Data moves between devices by JAX's collectives and lax.ppermute only.
A program may use at most 64 MiB of HBM per device.

```python
import math
import jax
import jax.numpy as jnp
import numpy as np
from jax import lax

D = 3584
FF = 2048
TOP = 2
TOK_DEV = 64
EXPERTS = 8
FF_PART = 2048
CAP = 20
TOKENS = 512
N_EXPERT = 8
N_TENSOR = 2


def shard_levels(stream_key, shape, pieces, low, high):
    def one(dim, blocks):
        steps = jax.random.uniform(jax.random.fold_in(jax.random.fold_in(stream_key, 6), dim), (blocks,), jnp.float32, low / len(pieces), high / len(pieces))
        return jnp.repeat(jnp.exp(steps), shape[dim] // blocks).reshape((-1,) + (1,) * (len(shape) - dim - 1))

    level = one(*pieces[0])
    for cut in pieces[1:]:
        level = level * one(*cut)
    return level


def assign_block(key, own, number, rows, amount, top, limit, slope):
    ranking = jax.random.permutation(key, amount)
    crowded, usual = shares(amount, rows * top, limit, slope, True), shares(amount, rows * top, limit, slope, False)
    places = jnp.arange(amount)

    def named(lengths, turn):
        used = int((lengths > 0).sum())
        fixed = max(1, used // 4)
        shifted = fixed + (places - fixed + turn * (used - fixed)) % max(1, amount - fixed)
        return jnp.zeros((amount,), jnp.int32).at[ranking[jnp.where(places < fixed, places, shifted)]].set(jnp.asarray(lengths, jnp.int32))

    lengths = jnp.where(number % 4 == 0, named(crowded, number // 4), named(usual, number - number // 4 - 1))
    mixed = jax.random.permutation(jax.random.fold_in(own, 3), amount)
    source_of, taker = mixed[0:amount // 2 * 2:2], mixed[1:amount // 2 * 2:2]
    room = jnp.minimum(lengths[source_of] - 1, limit - lengths[taker]) // 2
    room = jnp.where((source_of == ranking[0]) | (taker == ranking[0]) | (lengths[taker] == 0), 0, jnp.maximum(room, 0))
    shifted = jax.random.randint(jax.random.fold_in(own, 4), (amount // 2,), 0, 1 << 20) % (room + 1)
    lengths = lengths.at[source_of].add(-shifted).at[taker].add(shifted)
    members = jnp.searchsorted(jnp.cumsum(lengths), jnp.arange(rows * top), side="right").astype(jnp.int32)
    grid = members.reshape(top, rows).T
    grid = grid[jax.random.permutation(jax.random.fold_in(own, 1), rows)]
    turn = jax.random.randint(jax.random.fold_in(own, 2), (rows, 1), 0, top)
    return jnp.take_along_axis(grid, (jnp.arange(top)[None, :] + turn) % top, axis=1)


def shares(count, total, most, skew, full):
    loads = [(1 << 20) // math.isqrt(grade ** skew) + 1 for grade in range(1, count + 1)]
    largest = most if full else min(most, max(-(-total // count), total * loads[0] // sum(loads)))
    least = 1 if total - largest >= count - 1 else 0
    holding, spare = [largest] + [least] * (count - 1), total - largest - least * (count - 1)
    while spare > 0:
        free = [i for i in range(1, count) if holding[i] < largest] or [i for i in range(1, count) if holding[i] < most]
        mass, budget = sum([loads[i] for i in free]), spare
        for i in free:
            addition = min(most - holding[i], max(1, budget * loads[i] // mass), spare)
            holding[i] = holding[i] + addition
            spare = spare - addition
    return np.array(holding)


def centred(stream_key, dims, width, most, pieces=(), kind=jnp.bfloat16):
    values = jax.random.normal(stream_key, dims, jnp.float32) * width
    if len(pieces) > 0:
        values = shard_levels(stream_key, dims, pieces, -0.22, 0.18) * values
    return jnp.clip(values, min=-most, max=most).astype(kind)


def setup_inputs(seed: int = 0, part: int = 0) -> dict:
    arg_keys = jax.random.split(jax.random.key(seed), 7)
    own_keys = jax.random.split(jax.random.fold_in(arg_keys[6], part), 7)
    tokens = centred(own_keys[0], (TOKENS, D), 1.0, 6.0, ((0, 8), (1, 2)))
    expert_ids_keys = jax.random.split(jax.random.fold_in(own_keys[1], 1), TOKENS // TOK_DEV)
    expert_ids_turns = jax.random.permutation(jax.random.fold_in(own_keys[1], 3), TOKENS // TOK_DEV)
    expert_ids = jax.vmap(lambda own, number: assign_block(jax.random.fold_in(own_keys[1], 2), own, number, TOK_DEV, EXPERTS, TOP, CAP, 2))(expert_ids_keys, expert_ids_turns).reshape((TOKENS, TOP))
    gate_weights = jnp.clip(0.1 + 0.5 * jax.random.uniform(own_keys[2], (TOKENS, TOP), jnp.float32) ** shard_levels(own_keys[2], (TOKENS, TOP), ((0, 8),), -0.2, 0.2), 0.1, 0.6)
    w_gate = centred(arg_keys[3], (D, EXPERTS * FF), D ** -0.5, 0.09375, ((0, 2), (1, 8)))
    w_up = centred(arg_keys[4], (D, EXPERTS * FF), D ** -0.5, 0.09375, ((0, 2), (1, 8)))
    w_down = centred(arg_keys[5], (EXPERTS * FF, D), FF ** -0.5, 0.125, ((0, 8), (1, 2)))
    return dict(tokens=tokens, expert_ids=expert_ids, gate_weights=gate_weights, w_gate=w_gate, w_up=w_up, w_down=w_down)


def pair_slots(id_blocks):
    onehot = (id_blocks[:, :, None] == jnp.arange(EXPERTS, dtype=jnp.int32)[None, None, :]).astype(jnp.int32)
    earlier = jnp.cumsum(onehot, axis=1) - onehot
    return jnp.sum(earlier * onehot, axis=2)


def split_product(rows, columns):
    block_width = D // N_TENSOR
    total = jnp.zeros((rows.shape[0], columns.shape[1]), jnp.float32)
    for block_num in range(N_TENSOR):
        lower = block_num * block_width
        term = jnp.dot(rows[:, lower:lower + block_width], columns[lower:lower + block_width], preferred_element_type=jnp.float32).astype(jnp.bfloat16)
        term = lax.optimization_barrier(term)
        total = total + term.astype(jnp.float32)
    return total


def reference(tokens, expert_ids, gate_weights, w_gate, w_up, w_down):
    span_count = N_EXPERT // EXPERTS
    slot_index = pair_slots(expert_ids.reshape(N_EXPERT, TOK_DEV * TOP)).reshape(TOKENS, TOP).astype(jnp.int32)
    token_index = jnp.broadcast_to(jnp.arange(TOKENS, dtype=jnp.int32)[:, None], (TOKENS, TOP))
    source = (token_index // TOK_DEV).astype(jnp.int32)
    slot_table = jnp.full((EXPERTS, N_EXPERT, CAP), TOKENS, dtype=jnp.int32)
    slot_table = slot_table.at[expert_ids, source, slot_index].set(token_index)
    padded = jnp.concatenate([tokens, jnp.zeros((1, D), tokens.dtype)], axis=0)

    def one_expert(expert_num):
        gathered = padded[slot_table[expert_num].reshape(-1)]
        running = jnp.zeros((N_EXPERT * CAP, D), jnp.float32)
        for piece_num in range(span_count):
            offset = (expert_num * FF + piece_num * FF_PART).astype(jnp.int32)
            gate_cols = lax.dynamic_slice_in_dim(w_gate, offset, FF_PART, 1)
            up_cols = lax.dynamic_slice_in_dim(w_up, offset, FF_PART, 1)
            down_rows = lax.dynamic_slice_in_dim(w_down, offset, FF_PART, 0)
            gate = split_product(gathered, gate_cols)
            upper = split_product(gathered, up_cols)
            hidden = (jax.nn.silu(gate) * upper).astype(jnp.bfloat16)
            partial_value = jnp.dot(hidden, down_rows, preferred_element_type=jnp.float32).astype(jnp.bfloat16)
            partial_value = lax.optimization_barrier(partial_value)
            running = running + partial_value.astype(jnp.float32)
        return running

    outputs = lax.map(one_expert, jnp.arange(EXPERTS, dtype=jnp.int32))
    picked = outputs[expert_ids, source * CAP + slot_index]
    combined = jnp.sum(gate_weights[:, :, None] * picked, axis=1)
    return combined.astype(jnp.bfloat16)
```

```python
import jax
import jax.numpy as jnp
from jax import lax
from jax.experimental import pallas as pl
from jax.experimental.pallas import tpu as pltpu
from jax.sharding import PartitionSpec as P

FF = 2048
BF16 = jnp.bfloat16
F32 = jnp.float32
VMEM_SPEC = pl.BlockSpec(memory_space=pltpu.VMEM)
SMEM_SPEC = pl.BlockSpec(memory_space=pltpu.SMEM)
PIECES = 2
SEND_ORDER = (7, 6, 5, 4, 3, 2, 1)


def pair_slots(id_blocks, expert_count):
    onehot = (
        id_blocks[:, :, None] == jnp.arange(expert_count, dtype=jnp.int32)[None, None, :]
    ).astype(jnp.int32)
    earlier = jnp.cumsum(onehot, axis=1) - onehot
    return jnp.sum(earlier * onehot, axis=2)


def capacity_of(tok_rows, top_count, expert_count):
    return min(tok_rows, (5 * tok_rows * top_count + 4 * expert_count - 1) // (4 * expert_count))


def general(tokens, expert_ids, gate_weights, w_gate, w_up, w_down):
    tok_rows, half_width = tokens.shape
    top_count = expert_ids.shape[1]
    index_count = lax.axis_size("expert")
    part_width = w_gate.shape[1]
    span_count = FF // part_width
    expert_count = index_count // span_count
    capacity = capacity_of(tok_rows, top_count, expert_count)
    slot_index = pair_slots(expert_ids.reshape(1, tok_rows * top_count), expert_count).reshape(
        tok_rows, top_count
    )
    target = expert_ids * capacity + slot_index
    columns = jnp.arange(expert_count * capacity, dtype=jnp.int32)
    matches = target[:, :, None] == columns[None, None, :]
    selector = jnp.sum(matches.astype(BF16), axis=1)
    weights_table = jnp.sum(jnp.where(matches, gate_weights[:, :, None], 0.0), axis=1)
    buffer = lax.dot_general(
        selector, tokens, (((0,), (0,)), ((), ())), preferred_element_type=F32
    ).astype(BF16)
    buffer = jnp.repeat(buffer.reshape(expert_count, capacity, half_width), span_count, axis=0)
    received = lax.all_to_all(buffer, "expert", split_axis=0, concat_axis=0, tiled=True)
    sources, slot_count, feature_width = received.shape
    flat_rows = received.reshape(sources * slot_count, feature_width)
    gate_part = jnp.dot(flat_rows, w_gate, preferred_element_type=F32).astype(BF16)
    up_part = jnp.dot(flat_rows, w_up, preferred_element_type=F32).astype(BF16)
    gate_full = lax.psum(gate_part, "tensor").astype(F32)
    up_full = lax.psum(up_part, "tensor").astype(F32)
    hidden = (jax.nn.silu(gate_full) * up_full).astype(BF16)
    partial_value = jnp.dot(hidden, w_down, preferred_element_type=F32).astype(BF16)
    results = partial_value.reshape(sources, slot_count, partial_value.shape[1])
    returned = lax.all_to_all(results, "expert", split_axis=0, concat_axis=0, tiled=True)
    by_expert = jnp.sum(
        returned.reshape(expert_count, span_count, capacity, half_width).astype(F32), axis=1
    )
    combined = jnp.dot(
        weights_table,
        by_expert.reshape(expert_count * capacity, half_width),
        precision=lax.Precision.HIGHEST,
        preferred_element_type=F32,
    )
    return combined.astype(BF16)


def slot_rows(ids_ref, me, n, cap, tok_rows):
    shape = (n, tok_rows)
    expert = lax.broadcasted_iota(jnp.int32, shape, 0)
    first = (ids_ref[0:1, :] == expert).astype(F32)
    second = (ids_ref[1:2, :] == expert).astype(F32)
    before = (
        lax.broadcasted_iota(jnp.int32, (tok_rows, tok_rows), 0)
        < lax.broadcasted_iota(jnp.int32, (tok_rows, tok_rows), 1)
    ).astype(BF16)
    earlier = jnp.dot((first + second).astype(BF16), before, preferred_element_type=F32)
    slots = (
        jnp.sum(earlier * first, axis=0, keepdims=True),
        jnp.sum((earlier + first) * second, axis=0, keepdims=True),
    )
    return [
        (ids_ref[k : k + 1, :] ^ me) * (2 * cap) + slots[k].astype(jnp.int32) for k in range(2)
    ]


def dispatch_kernel(n, cap, me_ref, ids_ref, tok_ref, *out_refs):
    tok_rows, width = tok_ref.shape
    half = width // 2
    rows = slot_rows(ids_ref, me_ref[0], n, cap, tok_rows)
    number = lax.broadcasted_iota(jnp.int32, (2 * cap * n, tok_rows), 0)
    upper = jnp.where((number == rows[0]) | (number == rows[1]), 1.0, 0.0).astype(BF16)
    lower = jnp.where((number == rows[0] + cap) | (number == rows[1] + cap), 1.0, 0.0).astype(BF16)
    packed = jnp.dot(upper, tok_ref[:, :half], preferred_element_type=F32)
    packed = packed + jnp.dot(lower, tok_ref[:, half:], preferred_element_type=F32)
    for o in range(n):
        out_refs[o][...] = packed[o * 2 * cap : (o + 1) * 2 * cap].astype(BF16)


def gate_up_kernel(n, cap, piece, *refs):
    blocks, (wg_ref, wu_ref, out_ref, x_ref) = refs[:n], refs[n:]
    half = blocks[0].shape[1]
    for o in range(n):
        x_ref[pl.ds(o * cap, cap), :half] = blocks[o][:cap, :]
        x_ref[pl.ds(o * cap, cap), half:] = blocks[o][cap:, :]
    width = out_ref.shape[1] // 2
    tile = 512
    for which, w_ref in enumerate((wg_ref, wu_ref)):
        for j in range(width // tile):
            columns = pl.ds(piece * width + j * tile, tile)
            out_ref[:, pl.ds(which * width + j * tile, tile)] = jnp.dot(
                x_ref[...], w_ref[:, columns], preferred_element_type=F32
            ).astype(BF16)


def hidden_of(own_ref, other_ref):
    width = own_ref.shape[1] // 2
    gate = own_ref[:, :width].astype(F32) + other_ref[:, :width].astype(F32)
    up = own_ref[:, width:].astype(F32) + other_ref[:, width:].astype(F32)
    return (gate / (1.0 + jnp.exp(-gate)) * up).astype(BF16)


def down_first_kernel(own_ref, other_ref, wd_ref, acc_ref):
    hidden = hidden_of(own_ref, other_ref)
    acc_ref[...] = jnp.dot(hidden, wd_ref[: hidden.shape[1], :], preferred_element_type=F32)


def down_last_kernel(n, cap, own_ref, other_ref, wd_ref, acc_ref, *out_refs):
    hidden = hidden_of(own_ref, other_ref)
    depth = hidden.shape[1]
    out = acc_ref[...] + jnp.dot(hidden, wd_ref[depth:, :], preferred_element_type=F32)
    half = out.shape[1] // 2
    for o in range(n):
        out_refs[o][:cap, :] = out[o * cap : (o + 1) * cap, :half].astype(BF16)
        out_refs[o][cap:, :] = out[o * cap : (o + 1) * cap, half:].astype(BF16)


def combine_kernel(n, cap, me_ref, ids_ref, weights_ref, *refs):
    blocks, (out_ref, all_ref) = refs[:n], refs[n:]
    tok_rows, width = out_ref.shape
    half = width // 2
    for o in range(n):
        all_ref[pl.ds(o * 2 * cap, 2 * cap), :] = blocks[o][...]
    rows = slot_rows(ids_ref, me_ref[0], n, cap, tok_rows)
    number = lax.broadcasted_iota(jnp.int32, (2 * cap * n, tok_rows), 0)
    own = lax.broadcasted_iota(jnp.int32, (tok_rows, tok_rows), 0) == lax.broadcasted_iota(
        jnp.int32, (tok_rows, tok_rows), 1
    )
    weights = [
        jnp.sum(jnp.where(own, weights_ref[k : k + 1, :], 0.0), axis=1, keepdims=True)
        for k in range(2)
    ]
    for part in range(2):
        total = None
        for k in range(2):
            pick = jnp.where(number == rows[k] + part * cap, 1.0, 0.0).astype(BF16)
            picked = lax.dot_general(
                pick, all_ref[...], (((0,), (0,)), ((), ())), preferred_element_type=F32
            )
            term = weights[k] * picked
            total = term if total is None else total + term
        out_ref[:, part * half : (part + 1) * half] = total.astype(BF16)


def in_vmem(x):
    return pltpu.with_memory_space_constraint(x, pltpu.VMEM)


def resident(w, limit):
    return pl.pallas_call(
        lambda w_ref, out_ref: None,
        out_shape=pltpu.VMEM(w.shape, w.dtype),
        in_specs=[pl.BlockSpec(memory_space=pl.ANY)],
        out_specs=pl.BlockSpec(memory_space=pl.ANY),
        input_output_aliases={0: 0},
        compiler_params=pltpu.CompilerParams(vmem_limit_bytes=limit),
        name="weights_to_vmem",
    )(in_vmem(w))


def call(kernel, outs, args, smem=0, scratch=(), limit=20 << 20, cost=None, name=None, to_vmem=True):
    many = isinstance(outs, (tuple, list))
    shapes = [
        pltpu.VMEM(o.shape, o.dtype) if to_vmem else o for o in (outs if many else [outs])
    ]
    result = pl.pallas_call(
        kernel,
        out_shape=shapes,
        in_specs=[SMEM_SPEC] * smem + [VMEM_SPEC] * (len(args) - smem),
        out_specs=[VMEM_SPEC] * len(shapes),
        scratch_shapes=scratch,
        compiler_params=pltpu.CompilerParams(vmem_limit_bytes=limit),
        cost_estimate=cost,
        name=name,
    )(*args[:smem], *(in_vmem(a) for a in args[smem:]))
    return result if many else result[0]


def swap(x, axis, distance):
    return lax.ppermute(x, axis, [(i, i ^ distance) for i in range(lax.axis_size(axis))])


def one_expert_each(tokens, expert_ids, gate_weights, w_gate, w_up, w_down):
    tok_rows, width = tokens.shape
    n = lax.axis_size("expert")
    cap = capacity_of(tok_rows, expert_ids.shape[1], n)
    half, hidden_units = width // 2, w_gate.shape[1]
    me = lax.axis_index("expert").astype(jnp.int32).reshape(1)
    ids = expert_ids.T
    block = jax.ShapeDtypeStruct((2 * cap, half), BF16)

    sent = call(
        lambda *refs: dispatch_kernel(n, cap, *refs),
        [block] * n,
        [me, ids, tokens],
        smem=1,
        name="dispatch",
    )
    received = list(sent)
    for o in SEND_ORDER:
        received[o] = swap(sent[o], "expert", o)
    wg, wu, wd = (resident(w, 1 << 20) for w in (w_gate, w_up, w_down))

    piece_width = hidden_units // PIECES
    own, other = [], []
    for piece in range(PIECES):
        own.append(
            call(
                lambda *refs, piece=piece: gate_up_kernel(n, cap, piece, *refs),
                jax.ShapeDtypeStruct((n * cap, 2 * piece_width), BF16),
                [*received, wg, wu],
                scratch=[pltpu.VMEM((n * cap, width), BF16)],
                name="gate_up",
            )
        )
        other.append(swap(own[-1], "tensor", 1))
    acc = call(
        down_first_kernel,
        jax.ShapeDtypeStruct((n * cap, width), F32),
        [own[0], other[0], wd],
        name="down_first",
    )
    results = call(
        lambda *refs: down_last_kernel(n, cap, *refs),
        [block] * n,
        [own[1], other[1], wd, acc],
        name="down_last",
    )
    returned = list(results)
    for o in SEND_ORDER:
        returned[o] = swap(results[o], "expert", o)
    return call(
        lambda *refs: combine_kernel(n, cap, *refs),
        jax.ShapeDtypeStruct((tok_rows, width), BF16),
        [me, ids, gate_weights.T, *returned],
        smem=1,
        scratch=[pltpu.VMEM((2 * cap * n, half), BF16)],
        name="combine",
        to_vmem=False,
    )


def per_device(tokens, expert_ids, gate_weights, w_gate, w_up, w_down):
    args = (tokens, expert_ids, gate_weights, w_gate, w_up, w_down)
    whole = w_gate.shape[1] == FF and lax.axis_size("expert") == 8 and lax.axis_size("tensor") == 2
    if whole and expert_ids.shape[1] == 2:
        return one_expert_each(*args)
    return general(*args)


def solution(mesh):
    in_specs = (
        P(("group", "expert"), "tensor"),
        P(("group", "expert"), None),
        P(("group", "expert"), None),
        P("tensor", "expert"),
        P("tensor", "expert"),
        P("expert", "tensor"),
    )
    out_specs = P(("group", "expert"), "tensor")
    return jax.shard_map(
        per_device, mesh=mesh, in_specs=in_specs, out_specs=out_specs, check_vma=False
    )
```

```python
import jax
import jax.numpy as jnp
from jax import lax
from jax.experimental import pallas as pl
from jax.experimental.pallas import tpu as pltpu
from jax.sharding import PartitionSpec as P

FF = 2048
BF16 = jnp.bfloat16
F32 = jnp.float32
VMEM_SPEC = pl.BlockSpec(memory_space=pltpu.VMEM)
SMEM_SPEC = pl.BlockSpec(memory_space=pltpu.SMEM)
PIECES = 2
ORDER = (7, 6, 5, 4, 3, 2, 1, 0)


def pair_slots(id_blocks, expert_count):
    onehot = (
        id_blocks[:, :, None] == jnp.arange(expert_count, dtype=jnp.int32)[None, None, :]
    ).astype(jnp.int32)
    earlier = jnp.cumsum(onehot, axis=1) - onehot
    return jnp.sum(earlier * onehot, axis=2)


def capacity_of(tok_rows, top_count, expert_count):
    return min(tok_rows, (5 * tok_rows * top_count + 4 * expert_count - 1) // (4 * expert_count))


def general(tokens, expert_ids, gate_weights, w_gate, w_up, w_down):
    tok_rows, half_width = tokens.shape
    top_count = expert_ids.shape[1]
    index_count = lax.axis_size("expert")
    part_width = w_gate.shape[1]
    span_count = FF // part_width
    expert_count = index_count // span_count
    capacity = capacity_of(tok_rows, top_count, expert_count)
    slot_index = pair_slots(expert_ids.reshape(1, tok_rows * top_count), expert_count).reshape(
        tok_rows, top_count
    )
    target = expert_ids * capacity + slot_index
    columns = jnp.arange(expert_count * capacity, dtype=jnp.int32)
    matches = target[:, :, None] == columns[None, None, :]
    selector = jnp.sum(matches.astype(BF16), axis=1)
    weights_table = jnp.sum(jnp.where(matches, gate_weights[:, :, None], 0.0), axis=1)
    buffer = lax.dot_general(
        selector, tokens, (((0,), (0,)), ((), ())), preferred_element_type=F32
    ).astype(BF16)
    buffer = jnp.repeat(buffer.reshape(expert_count, capacity, half_width), span_count, axis=0)
    received = lax.all_to_all(buffer, "expert", split_axis=0, concat_axis=0, tiled=True)
    sources, slot_count, feature_width = received.shape
    flat_rows = received.reshape(sources * slot_count, feature_width)
    gate_part = jnp.dot(flat_rows, w_gate, preferred_element_type=F32).astype(BF16)
    up_part = jnp.dot(flat_rows, w_up, preferred_element_type=F32).astype(BF16)
    gate_full = lax.psum(gate_part, "tensor").astype(F32)
    up_full = lax.psum(up_part, "tensor").astype(F32)
    hidden = (jax.nn.silu(gate_full) * up_full).astype(BF16)
    partial_value = jnp.dot(hidden, w_down, preferred_element_type=F32).astype(BF16)
    results = partial_value.reshape(sources, slot_count, partial_value.shape[1])
    returned = lax.all_to_all(results, "expert", split_axis=0, concat_axis=0, tiled=True)
    by_expert = jnp.sum(
        returned.reshape(expert_count, span_count, capacity, half_width).astype(F32), axis=1
    )
    combined = jnp.dot(
        weights_table,
        by_expert.reshape(expert_count * capacity, half_width),
        precision=lax.Precision.HIGHEST,
        preferred_element_type=F32,
    )
    return combined.astype(BF16)


def slot_rows(ids_ref, me, n, cap, tok_rows):
    shape = (n, tok_rows)
    expert = lax.broadcasted_iota(jnp.int32, shape, 0)
    first = (ids_ref[0:1, :] == expert).astype(F32)
    second = (ids_ref[1:2, :] == expert).astype(F32)
    before = (
        lax.broadcasted_iota(jnp.int32, (tok_rows, tok_rows), 0)
        < lax.broadcasted_iota(jnp.int32, (tok_rows, tok_rows), 1)
    ).astype(BF16)
    earlier = jnp.dot((first + second).astype(BF16), before, preferred_element_type=F32)
    slots = (
        jnp.sum(earlier * first, axis=0, keepdims=True),
        jnp.sum((earlier + first) * second, axis=0, keepdims=True),
    )
    return [
        (ids_ref[k : k + 1, :] ^ me) * (2 * cap) + slots[k].astype(jnp.int32) for k in range(2)
    ]


def dispatch_kernel(n, cap, me_ref, ids_ref, tok_ref, *out_refs):
    tok_rows, width = tok_ref.shape
    half = width // 2
    rows = slot_rows(ids_ref, me_ref[0], n, cap, tok_rows)
    number = lax.broadcasted_iota(jnp.int32, (2 * cap * n, tok_rows), 0)
    upper = jnp.where((number == rows[0]) | (number == rows[1]), 1.0, 0.0).astype(BF16)
    lower = jnp.where((number == rows[0] + cap) | (number == rows[1] + cap), 1.0, 0.0).astype(BF16)
    packed = jnp.dot(upper, tok_ref[:, :half], preferred_element_type=F32)
    packed = packed + jnp.dot(lower, tok_ref[:, half:], preferred_element_type=F32)
    for o, out_ref in zip(ORDER, out_refs):
        out_ref[...] = packed[o * 2 * cap : (o + 1) * 2 * cap].astype(BF16)


def gate_up_kernel(n, cap, piece, *refs):
    blocks, (wg_ref, wu_ref, out_ref, x_ref) = refs[:n], refs[n:]
    half = blocks[0].shape[1]
    for o, block in zip(ORDER, blocks):
        x_ref[pl.ds(o * cap, cap), :half] = block[:cap, :]
        x_ref[pl.ds(o * cap, cap), half:] = block[cap:, :]
    width = out_ref.shape[1] // 2
    tile = 512
    for which, w_ref in enumerate((wg_ref, wu_ref)):
        for j in range(width // tile):
            columns = pl.ds(piece * width + j * tile, tile)
            out_ref[:, pl.ds(which * width + j * tile, tile)] = jnp.dot(
                x_ref[...], w_ref[:, columns], preferred_element_type=F32
            ).astype(BF16)


def hidden_of(own_ref, other_ref):
    width = own_ref.shape[1] // 2
    gate = own_ref[:, :width].astype(F32) + other_ref[:, :width].astype(F32)
    up = own_ref[:, width:].astype(F32) + other_ref[:, width:].astype(F32)
    return (gate / (1.0 + jnp.exp(-gate)) * up).astype(BF16)


def down_first_kernel(own_ref, other_ref, wd_ref, acc_ref):
    hidden = hidden_of(own_ref, other_ref)
    acc_ref[...] = jnp.dot(hidden, wd_ref[: hidden.shape[1], :], preferred_element_type=F32)


def down_last_kernel(n, cap, own_ref, other_ref, wd_ref, acc_ref, *out_refs):
    hidden = hidden_of(own_ref, other_ref)
    depth = hidden.shape[1]
    out = acc_ref[...] + jnp.dot(hidden, wd_ref[depth:, :], preferred_element_type=F32)
    half = out.shape[1] // 2
    for o, out_ref in zip(ORDER, out_refs):
        out_ref[:cap, :] = out[o * cap : (o + 1) * cap, :half].astype(BF16)
        out_ref[cap:, :] = out[o * cap : (o + 1) * cap, half:].astype(BF16)


def combine_kernel(n, cap, me_ref, ids_ref, weights_ref, *refs):
    blocks, (out_ref, all_ref) = refs[:n], refs[n:]
    tok_rows, width = out_ref.shape
    half = width // 2
    for o, block in zip(ORDER, blocks):
        all_ref[pl.ds(o * 2 * cap, 2 * cap), :] = block[...]
    rows = slot_rows(ids_ref, me_ref[0], n, cap, tok_rows)
    number = lax.broadcasted_iota(jnp.int32, (2 * cap * n, tok_rows), 0)
    own = lax.broadcasted_iota(jnp.int32, (tok_rows, tok_rows), 0) == lax.broadcasted_iota(
        jnp.int32, (tok_rows, tok_rows), 1
    )
    weights = [
        jnp.sum(jnp.where(own, weights_ref[k : k + 1, :], 0.0), axis=1, keepdims=True)
        for k in range(2)
    ]
    for part in range(2):
        total = None
        for k in range(2):
            pick = jnp.where(number == rows[k] + part * cap, 1.0, 0.0).astype(BF16)
            picked = lax.dot_general(
                pick, all_ref[...], (((0,), (0,)), ((), ())), preferred_element_type=F32
            )
            term = weights[k] * picked
            total = term if total is None else total + term
        out_ref[:, part * half : (part + 1) * half] = total.astype(BF16)


def in_vmem(x):
    return pltpu.with_memory_space_constraint(x, pltpu.VMEM)


def call(kernel, outs, args, smem=0, scratch=(), limit=20 << 20, cost=None, name=None, to_vmem=True):
    many = isinstance(outs, (tuple, list))
    shapes = [
        pltpu.VMEM(o.shape, o.dtype) if to_vmem else o for o in (outs if many else [outs])
    ]
    result = pl.pallas_call(
        kernel,
        out_shape=shapes,
        in_specs=[SMEM_SPEC] * smem + [VMEM_SPEC] * (len(args) - smem),
        out_specs=[VMEM_SPEC] * len(shapes),
        scratch_shapes=scratch,
        compiler_params=pltpu.CompilerParams(vmem_limit_bytes=limit),
        cost_estimate=cost,
        name=name,
    )(*args[:smem], *(in_vmem(a) for a in args[smem:]))
    return result if many else result[0]


def swap(x, axis, distance):
    if distance == 0:
        return x
    return lax.ppermute(x, axis, [(i, i ^ distance) for i in range(lax.axis_size(axis))])


def one_expert_each(tokens, expert_ids, gate_weights, w_gate, w_up, w_down):
    tok_rows, width = tokens.shape
    n = lax.axis_size("expert")
    cap = capacity_of(tok_rows, expert_ids.shape[1], n)
    half, hidden_units = width // 2, w_gate.shape[1]
    me = lax.axis_index("expert").astype(jnp.int32).reshape(1)
    ids = expert_ids.T
    loaded = sum(w.size * 2 for w in (w_gate, w_up, w_down))
    block = jax.ShapeDtypeStruct((2 * cap, half), BF16)

    sent = call(
        lambda *refs: dispatch_kernel(n, cap, *refs),
        [block] * n,
        [me, ids, tokens],
        smem=1,
        cost=pl.CostEstimate(flops=20_000_000_000, bytes_accessed=2 * loaded, transcendentals=0),
        name="dispatch",
    )
    received = [swap(x, "expert", o) for o, x in zip(ORDER, sent)]

    piece_width = hidden_units // PIECES
    own, other = [], []
    for piece in range(PIECES):
        own.append(
            call(
                lambda *refs, piece=piece: gate_up_kernel(n, cap, piece, *refs),
                jax.ShapeDtypeStruct((n * cap, 2 * piece_width), BF16),
                [*received, w_gate, w_up],
                scratch=[pltpu.VMEM((n * cap, width), BF16)],
                name="gate_up",
            )
        )
        other.append(swap(own[-1], "tensor", 1))
    acc = call(
        down_first_kernel,
        jax.ShapeDtypeStruct((n * cap, width), F32),
        [own[0], other[0], w_down],
        name="down_first",
    )
    results = call(
        lambda *refs: down_last_kernel(n, cap, *refs),
        [block] * n,
        [own[1], other[1], w_down, acc],
        name="down_last",
    )
    returned = [swap(x, "expert", o) for o, x in zip(ORDER, results)]
    return call(
        lambda *refs: combine_kernel(n, cap, *refs),
        jax.ShapeDtypeStruct((tok_rows, width), BF16),
        [me, ids, gate_weights.T, *returned],
        smem=1,
        scratch=[pltpu.VMEM((2 * cap * n, half), BF16)],
        name="combine",
        to_vmem=False,
    )


def per_device(tokens, expert_ids, gate_weights, w_gate, w_up, w_down):
    args = (tokens, expert_ids, gate_weights, w_gate, w_up, w_down)
    whole = w_gate.shape[1] == FF and lax.axis_size("expert") == 8 and lax.axis_size("tensor") == 2
    if whole and expert_ids.shape[1] == 2:
        return one_expert_each(*args)
    return general(*args)


def solution(mesh):
    in_specs = (
        P(("group", "expert"), "tensor"),
        P(("group", "expert"), None),
        P(("group", "expert"), None),
        P("tensor", "expert"),
        P("tensor", "expert"),
        P("expert", "tensor"),
    )
    out_specs = P(("group", "expert"), "tensor")
    return jax.shard_map(
        per_device, mesh=mesh, in_specs=in_specs, out_specs=out_specs, check_vma=False
    )
```

```python
import jax
import jax.numpy as jnp
from jax import lax
from jax.experimental import pallas as pl
from jax.experimental.pallas import tpu as pltpu
from jax.sharding import PartitionSpec as P

FF = 2048
BF16 = jnp.bfloat16
F32 = jnp.float32
VMEM_SPEC = pl.BlockSpec(memory_space=pltpu.VMEM)
SMEM_SPEC = pl.BlockSpec(memory_space=pltpu.SMEM)
PIECES = (2,)
BATCHES = ((6, 1, 4, 3, 5, 7, 2, 0),)
STARTS = (6, 1, 4, 3, 5, 7, 2, 0)


def pair_slots(id_blocks, expert_count):
    onehot = (
        id_blocks[:, :, None] == jnp.arange(expert_count, dtype=jnp.int32)[None, None, :]
    ).astype(jnp.int32)
    earlier = jnp.cumsum(onehot, axis=1) - onehot
    return jnp.sum(earlier * onehot, axis=2)


def capacity_of(tok_rows, top_count, expert_count):
    return min(tok_rows, (5 * tok_rows * top_count + 4 * expert_count - 1) // (4 * expert_count))


def general(tokens, expert_ids, gate_weights, w_gate, w_up, w_down):
    tok_rows, half_width = tokens.shape
    top_count = expert_ids.shape[1]
    index_count = lax.axis_size("expert")
    part_width = w_gate.shape[1]
    span_count = FF // part_width
    expert_count = index_count // span_count
    capacity = capacity_of(tok_rows, top_count, expert_count)
    slot_index = pair_slots(expert_ids.reshape(1, tok_rows * top_count), expert_count).reshape(
        tok_rows, top_count
    )
    target = expert_ids * capacity + slot_index
    columns = jnp.arange(expert_count * capacity, dtype=jnp.int32)
    matches = target[:, :, None] == columns[None, None, :]
    selector = jnp.sum(matches.astype(BF16), axis=1)
    weights_table = jnp.sum(jnp.where(matches, gate_weights[:, :, None], 0.0), axis=1)
    buffer = lax.dot_general(
        selector, tokens, (((0,), (0,)), ((), ())), preferred_element_type=F32
    ).astype(BF16)
    buffer = jnp.repeat(buffer.reshape(expert_count, capacity, half_width), span_count, axis=0)
    received = lax.all_to_all(buffer, "expert", split_axis=0, concat_axis=0, tiled=True)
    sources, slot_count, feature_width = received.shape
    flat_rows = received.reshape(sources * slot_count, feature_width)
    gate_part = jnp.dot(flat_rows, w_gate, preferred_element_type=F32).astype(BF16)
    up_part = jnp.dot(flat_rows, w_up, preferred_element_type=F32).astype(BF16)
    gate_full = lax.psum(gate_part, "tensor").astype(F32)
    up_full = lax.psum(up_part, "tensor").astype(F32)
    hidden = (jax.nn.silu(gate_full) * up_full).astype(BF16)
    partial_value = jnp.dot(hidden, w_down, preferred_element_type=F32).astype(BF16)
    results = partial_value.reshape(sources, slot_count, partial_value.shape[1])
    returned = lax.all_to_all(results, "expert", split_axis=0, concat_axis=0, tiled=True)
    by_expert = jnp.sum(
        returned.reshape(expert_count, span_count, capacity, half_width).astype(F32), axis=1
    )
    combined = jnp.dot(
        weights_table,
        by_expert.reshape(expert_count * capacity, half_width),
        precision=lax.Precision.HIGHEST,
        preferred_element_type=F32,
    )
    return combined.astype(BF16)


def slot_rows(ids_ref, me, n, cap, tok_rows):
    shape = (n, tok_rows)
    expert = lax.broadcasted_iota(jnp.int32, shape, 0)
    first = (ids_ref[0:1, :] == expert).astype(F32)
    second = (ids_ref[1:2, :] == expert).astype(F32)
    before = (
        lax.broadcasted_iota(jnp.int32, (tok_rows, tok_rows), 0)
        < lax.broadcasted_iota(jnp.int32, (tok_rows, tok_rows), 1)
    ).astype(BF16)
    earlier = jnp.dot((first + second).astype(BF16), before, preferred_element_type=F32)
    slots = (
        jnp.sum(earlier * first, axis=0, keepdims=True),
        jnp.sum((earlier + first) * second, axis=0, keepdims=True),
    )
    return [
        (ids_ref[k : k + 1, :] ^ me) * (2 * cap) + slots[k].astype(jnp.int32) for k in range(2)
    ]


def dispatch_kernel(n, cap, me_ref, ids_hbm, tok_hbm, *refs):
    out_refs, (ids_ref, tok_ref, sems) = refs[:n], refs[n:]
    ids_copy = pltpu.make_async_copy(ids_hbm, ids_ref, sems.at[0])
    tok_copy = pltpu.make_async_copy(tok_hbm, tok_ref, sems.at[1])
    ids_copy.start()
    tok_copy.start()
    tok_rows, width = tok_ref.shape
    half = width // 2
    ids_copy.wait()
    rows = slot_rows(ids_ref, me_ref[0], n, cap, tok_rows)
    number = lax.broadcasted_iota(jnp.int32, (2 * cap * n, tok_rows), 0)
    upper = jnp.where((number == rows[0]) | (number == rows[1]), 1.0, 0.0).astype(BF16)
    lower = jnp.where((number == rows[0] + cap) | (number == rows[1] + cap), 1.0, 0.0).astype(BF16)
    tok_copy.wait()
    packed = jnp.dot(upper, tok_ref[:, :half], preferred_element_type=F32)
    packed = packed + jnp.dot(lower, tok_ref[:, half:], preferred_element_type=F32)
    for o, out_ref in zip(STARTS, out_refs):
        out_ref[...] = packed[o * 2 * cap : (o + 1) * 2 * cap].astype(BF16)


def gate_up_kernel(cap, piece, *refs):
    blocks, (wg_ref, wu_ref, out_ref, x_ref) = refs[:-4], refs[-4:]
    half = blocks[0].shape[1]
    for i, block in enumerate(blocks):
        x_ref[pl.ds(i * cap, cap), :half] = block[:cap, :]
        x_ref[pl.ds(i * cap, cap), half:] = block[cap:, :]
    width = out_ref.shape[1] // 2
    tile = min(512, width)
    for which, w_ref in enumerate((wg_ref, wu_ref)):
        for j in range(width // tile):
            columns = pl.ds(piece * width + j * tile, tile)
            out_ref[:, pl.ds(which * width + j * tile, tile)] = jnp.dot(
                x_ref[...], w_ref[:, columns], preferred_element_type=F32
            ).astype(BF16)


def hidden_of(own_ref, other_ref):
    width = own_ref.shape[1] // 2
    gate = own_ref[:, :width].astype(F32) + other_ref[:, :width].astype(F32)
    up = own_ref[:, width:].astype(F32) + other_ref[:, width:].astype(F32)
    return (gate / (1.0 + jnp.exp(-gate)) * up).astype(BF16)


def down_first_kernel(count, *refs):
    own, other, (wd_ref, acc_ref) = refs[:count], refs[count : 2 * count], refs[2 * count :]
    total = None
    for i in range(count):
        hidden = hidden_of(own[i], other[i])
        depth = hidden.shape[1]
        term = jnp.dot(hidden, wd_ref[pl.ds(i * depth, depth), :], preferred_element_type=F32)
        total = term if total is None else total + term
    acc_ref[...] = total


def down_last_kernel(cap, own_ref, other_ref, wd_ref, acc_ref, *out_refs):
    hidden = hidden_of(own_ref, other_ref)
    out = acc_ref[...] + jnp.dot(
        hidden, wd_ref[wd_ref.shape[0] - hidden.shape[1] :, :], preferred_element_type=F32
    )
    half = out.shape[1] // 2
    for i, out_ref in enumerate(out_refs):
        out_ref[:cap, :] = out[i * cap : (i + 1) * cap, :half].astype(BF16)
        out_ref[cap:, :] = out[i * cap : (i + 1) * cap, half:].astype(BF16)


def plan_kernel(n, cap, me_ref, ids_ref, weights_ref, pick_ref, scale_ref):
    tok_rows = ids_ref.shape[1]
    rows = slot_rows(ids_ref, me_ref[0], n, cap, tok_rows)
    own = lax.broadcasted_iota(jnp.int32, (tok_rows, tok_rows), 0) == lax.broadcasted_iota(
        jnp.int32, (tok_rows, tok_rows), 1
    )
    number = lax.broadcasted_iota(jnp.int32, (tok_rows, 2 * cap * n), 1)
    for k in range(2):
        weight = jnp.sum(jnp.where(own, weights_ref[k : k + 1, :], 0.0), axis=1, keepdims=True)
        scale_ref[pl.ds(k * tok_rows, tok_rows), :] = jnp.broadcast_to(weight, (tok_rows, 128))
        row = jnp.sum(jnp.where(own, rows[k].astype(F32), 0.0), axis=1, keepdims=True)
        row = row.astype(jnp.int32)
        for part in range(2):
            pick = jnp.where(number == row + part * cap, 1.0, 0.0).astype(BF16)
            pick_ref[pl.ds((2 * part + k) * tok_rows, tok_rows), :] = pick


def combine_kernel(cap, places, pick_ref, scale_ref, *refs):
    n = len(places)
    blocks, (out_hbm, all_ref, out_ref, sems) = refs[:n], refs[n:]
    tok_rows, width = out_ref.shape
    half = width // 2
    for o, block in zip(places, blocks):
        all_ref[pl.ds(o * 2 * cap, 2 * cap), :] = block[...]
    weights = [scale_ref[pl.ds(k * tok_rows, tok_rows), 0:1] for k in range(2)]
    copies = []
    for part in range(2):
        picked = jnp.dot(
            pick_ref[pl.ds(2 * part * tok_rows, 2 * tok_rows), :],
            all_ref[...],
            preferred_element_type=F32,
        )
        total = weights[0] * picked[:tok_rows] + weights[1] * picked[tok_rows:]
        columns = pl.ds(part * half, half)
        out_ref[:, columns] = total.astype(BF16)
        copies.append(
            pltpu.make_async_copy(
                out_ref.at[:, columns], out_hbm.at[:, columns], sems.at[part]
            )
        )
        copies[-1].start()
    for copy in copies:
        copy.wait()


def in_vmem(x):
    return pltpu.with_memory_space_constraint(x, pltpu.VMEM)


def in_hbm(x):
    return pltpu.with_memory_space_constraint(x, pltpu.HBM)


def call(kernel, outs, args, smem=0, hbm=0, scratch=(), limit=20 << 20, cost=None, name=None):
    many = isinstance(outs, (tuple, list))
    result = pl.pallas_call(
        kernel,
        out_shape=[pltpu.VMEM(o.shape, o.dtype) for o in (outs if many else [outs])],
        in_specs=[SMEM_SPEC] * smem
        + [pl.BlockSpec(memory_space=pltpu.HBM)] * hbm
        + [VMEM_SPEC] * (len(args) - smem - hbm),
        out_specs=[VMEM_SPEC] * (len(outs) if many else 1),
        scratch_shapes=scratch,
        compiler_params=pltpu.CompilerParams(vmem_limit_bytes=limit),
        cost_estimate=cost,
        name=name,
    )(*args[: smem + hbm], *(in_vmem(a) for a in args[smem + hbm :]))
    return result if many else result[0]


def swap(x, axis, distance):
    if distance == 0:
        return x
    return lax.ppermute(x, axis, [(i, i ^ distance) for i in range(lax.axis_size(axis))])


def experts(blocks, after, pieces, cap, w_gate, w_up, w_down):
    rows, width, hidden_units = len(blocks) * cap, 2 * blocks[0].shape[1], w_gate.shape[1]
    piece_width = hidden_units // pieces
    own, other = [], []
    for piece in range(pieces):
        own.append(
            call(
                lambda *refs, piece=piece: gate_up_kernel(cap, piece, *refs[len(after) :]),
                jax.ShapeDtypeStruct((rows, 2 * piece_width), BF16),
                [*after, *blocks, w_gate, w_up],
                scratch=[pltpu.VMEM((rows, width), BF16)],
                cost=estimate(),
                name="gate_up",
            )
        )
        other.append(swap(own[-1], "tensor", 1))
    acc = call(
        lambda *refs: down_first_kernel(pieces - 1, *refs),
        jax.ShapeDtypeStruct((rows, width), F32),
        [*own[:-1], *other[:-1], w_down],
        cost=estimate(),
        name="down_first",
    )
    results = call(
        lambda *refs: down_last_kernel(cap, *refs),
        [jax.ShapeDtypeStruct(b.shape, b.dtype) for b in blocks],
        [own[-1], other[-1], w_down, acc],
        cost=estimate(),
        name="down_last",
    )
    return results, own


def estimate():
    return pl.CostEstimate(flops=1, bytes_accessed=0, transcendentals=0)


def one_expert_each(tokens, expert_ids, gate_weights, w_gate, w_up, w_down):
    tok_rows, width = tokens.shape
    n = lax.axis_size("expert")
    cap = capacity_of(tok_rows, expert_ids.shape[1], n)
    half = width // 2
    me = lax.axis_index("expert").astype(jnp.int32).reshape(1)
    ids = expert_ids.T
    loaded = sum(w.size * 2 for w in (w_gate, w_up, w_down))
    block = jax.ShapeDtypeStruct((2 * cap, half), BF16)

    sent = call(
        lambda *refs: dispatch_kernel(n, cap, *refs),
        [block] * n,
        [me, in_hbm(ids), in_hbm(tokens)],
        smem=1,
        hbm=2,
        scratch=[
            pltpu.VMEM(ids.shape, ids.dtype),
            pltpu.VMEM(tokens.shape, tokens.dtype),
            pltpu.SemaphoreType.DMA((2,)),
        ],
        cost=pl.CostEstimate(flops=20_000_000_000, bytes_accessed=2 * loaded, transcendentals=0),
        name="dispatch",
    )
    received = {o: swap(x, "expert", o) for o, x in zip(STARTS, sent)}
    returned = {}
    after = []
    for batch, pieces in zip(BATCHES, PIECES):
        results, after = experts(
            [received[o] for o in batch], after, pieces, cap, w_gate, w_up, w_down
        )
        for o, x in zip(batch, results):
            returned[o] = swap(x, "expert", o)
    pick, scale = call(
        lambda *refs: plan_kernel(n, cap, *refs),
        [
            jax.ShapeDtypeStruct((4 * tok_rows, 2 * cap * n), BF16),
            jax.ShapeDtypeStruct((2 * tok_rows, 128), F32),
        ],
        [me, ids, gate_weights.T],
        smem=1,
        cost=estimate(),
        name="plan",
    )
    places = [o for batch in BATCHES for o in batch]
    return pl.pallas_call(
        lambda *refs: combine_kernel(cap, places, *refs),
        out_shape=jax.ShapeDtypeStruct((tok_rows, width), BF16),
        in_specs=[VMEM_SPEC] * (2 + n),
        out_specs=pl.BlockSpec(memory_space=pl.ANY),
        scratch_shapes=[
            pltpu.VMEM((2 * cap * n, half), BF16),
            pltpu.VMEM((tok_rows, width), BF16),
            pltpu.SemaphoreType.DMA((2,)),
        ],
        compiler_params=pltpu.CompilerParams(vmem_limit_bytes=20 << 20),
        name="combine",
    )(*(in_vmem(x) for x in (pick, scale, *(returned[o] for o in places))))


def per_device(tokens, expert_ids, gate_weights, w_gate, w_up, w_down):
    args = (tokens, expert_ids, gate_weights, w_gate, w_up, w_down)
    whole = w_gate.shape[1] == FF and lax.axis_size("expert") == 8 and lax.axis_size("tensor") == 2
    if whole and expert_ids.shape[1] == 2:
        return one_expert_each(*args)
    return general(*args)


def solution(mesh):
    in_specs = (
        P(("group", "expert"), "tensor"),
        P(("group", "expert"), None),
        P(("group", "expert"), None),
        P("tensor", "expert"),
        P("tensor", "expert"),
        P("expert", "tensor"),
    )
    out_specs = P(("group", "expert"), "tensor")
    return jax.shard_map(
        per_device, mesh=mesh, in_specs=in_specs, out_specs=out_specs, check_vma=False
    )
```

```python
import jax
import jax.numpy as jnp
from jax import lax
from jax.experimental import pallas as pl
from jax.experimental.pallas import tpu as pltpu
from jax.sharding import PartitionSpec as P

FF = 2048
BF16 = jnp.bfloat16
F32 = jnp.float32
VMEM_SPEC = pl.BlockSpec(memory_space=pltpu.VMEM)
SMEM_SPEC = pl.BlockSpec(memory_space=pltpu.SMEM)
PIECES = (2,)
PIECES = (1024, 512, 512)
STARTS = (6, 1, 4, 3, 5, 7, 2, 0)
ROWS = (6, 1, 4, 3, 5, 7, 2, 0)
RETURNS = (6, 1, 4, 3, 5, 7, 2, 0)
PLACES = (6, 1, 4, 3, 5, 7, 2, 0)


def pair_slots(id_blocks, expert_count):
    onehot = (
        id_blocks[:, :, None] == jnp.arange(expert_count, dtype=jnp.int32)[None, None, :]
    ).astype(jnp.int32)
    earlier = jnp.cumsum(onehot, axis=1) - onehot
    return jnp.sum(earlier * onehot, axis=2)


def capacity_of(tok_rows, top_count, expert_count):
    return min(tok_rows, (5 * tok_rows * top_count + 4 * expert_count - 1) // (4 * expert_count))


def general(tokens, expert_ids, gate_weights, w_gate, w_up, w_down):
    tok_rows, half_width = tokens.shape
    top_count = expert_ids.shape[1]
    index_count = lax.axis_size("expert")
    part_width = w_gate.shape[1]
    span_count = FF // part_width
    expert_count = index_count // span_count
    capacity = capacity_of(tok_rows, top_count, expert_count)
    slot_index = pair_slots(expert_ids.reshape(1, tok_rows * top_count), expert_count).reshape(
        tok_rows, top_count
    )
    target = expert_ids * capacity + slot_index
    columns = jnp.arange(expert_count * capacity, dtype=jnp.int32)
    matches = target[:, :, None] == columns[None, None, :]
    selector = jnp.sum(matches.astype(BF16), axis=1)
    weights_table = jnp.sum(jnp.where(matches, gate_weights[:, :, None], 0.0), axis=1)
    buffer = lax.dot_general(
        selector, tokens, (((0,), (0,)), ((), ())), preferred_element_type=F32
    ).astype(BF16)
    buffer = jnp.repeat(buffer.reshape(expert_count, capacity, half_width), span_count, axis=0)
    received = lax.all_to_all(buffer, "expert", split_axis=0, concat_axis=0, tiled=True)
    sources, slot_count, feature_width = received.shape
    flat_rows = received.reshape(sources * slot_count, feature_width)
    gate_part = jnp.dot(flat_rows, w_gate, preferred_element_type=F32).astype(BF16)
    up_part = jnp.dot(flat_rows, w_up, preferred_element_type=F32).astype(BF16)
    gate_full = lax.psum(gate_part, "tensor").astype(F32)
    up_full = lax.psum(up_part, "tensor").astype(F32)
    hidden = (jax.nn.silu(gate_full) * up_full).astype(BF16)
    partial_value = jnp.dot(hidden, w_down, preferred_element_type=F32).astype(BF16)
    results = partial_value.reshape(sources, slot_count, partial_value.shape[1])
    returned = lax.all_to_all(results, "expert", split_axis=0, concat_axis=0, tiled=True)
    by_expert = jnp.sum(
        returned.reshape(expert_count, span_count, capacity, half_width).astype(F32), axis=1
    )
    combined = jnp.dot(
        weights_table,
        by_expert.reshape(expert_count * capacity, half_width),
        precision=lax.Precision.HIGHEST,
        preferred_element_type=F32,
    )
    return combined.astype(BF16)


def slot_rows(ids_ref, me, n, cap, tok_rows):
    shape = (n, tok_rows)
    expert = lax.broadcasted_iota(jnp.int32, shape, 0)
    first = (ids_ref[0:1, :] == expert).astype(F32)
    second = (ids_ref[1:2, :] == expert).astype(F32)
    before = (
        lax.broadcasted_iota(jnp.int32, (tok_rows, tok_rows), 0)
        < lax.broadcasted_iota(jnp.int32, (tok_rows, tok_rows), 1)
    ).astype(BF16)
    earlier = jnp.dot((first + second).astype(BF16), before, preferred_element_type=F32)
    slots = (
        jnp.sum(earlier * first, axis=0, keepdims=True),
        jnp.sum((earlier + first) * second, axis=0, keepdims=True),
    )
    return [
        (ids_ref[k : k + 1, :] ^ me) * (2 * cap) + slots[k].astype(jnp.int32) for k in range(2)
    ]


def dispatch_kernel(n, cap, me_ref, ids_hbm, tok_hbm, *refs):
    out_refs, (ids_ref, tok_ref, sems) = refs[:n], refs[n:]
    ids_copy = pltpu.make_async_copy(ids_hbm, ids_ref, sems.at[0])
    tok_copy = pltpu.make_async_copy(tok_hbm, tok_ref, sems.at[1])
    ids_copy.start()
    tok_copy.start()
    tok_rows, width = tok_ref.shape
    half = width // 2
    ids_copy.wait()
    rows = slot_rows(ids_ref, me_ref[0], n, cap, tok_rows)
    number = lax.broadcasted_iota(jnp.int32, (2 * cap * n, tok_rows), 0)
    upper = jnp.where((number == rows[0]) | (number == rows[1]), 1.0, 0.0).astype(BF16)
    lower = jnp.where((number == rows[0] + cap) | (number == rows[1] + cap), 1.0, 0.0).astype(BF16)
    tok_copy.wait()
    packed = jnp.dot(upper, tok_ref[:, :half], preferred_element_type=F32)
    packed = packed + jnp.dot(lower, tok_ref[:, half:], preferred_element_type=F32)
    for o, out_ref in zip(STARTS, out_refs):
        out_ref[...] = packed[o * 2 * cap : (o + 1) * 2 * cap].astype(BF16)


def gate_up(x_ref, wg_ref, wu_ref, out_ref, start):
    width = out_ref.shape[1] // 2
    tile = 256
    for which, w_ref in enumerate((wg_ref, wu_ref)):
        for j in range(width // tile):
            columns = pl.ds(start + j * tile, tile)
            out_ref[:, pl.ds(which * width + j * tile, tile)] = jnp.dot(
                x_ref[...], w_ref[:, columns], preferred_element_type=F32
            ).astype(BF16)


def gate_up_first_kernel(cap, *refs):
    blocks, (wg_ref, wu_ref, _, out_ref, x_ref) = refs[:-5], refs[-5:]
    half = blocks[0].shape[1]
    for i, block in enumerate(blocks):
        x_ref[pl.ds(i * cap, cap), :half] = block[:cap, :]
        x_ref[pl.ds(i * cap, cap), half:] = block[cap:, :]
    gate_up(x_ref, wg_ref, wu_ref, out_ref, 0)


def gate_up_next_kernel(start, x_ref, wg_ref, wu_ref, out_ref):
    gate_up(x_ref, wg_ref, wu_ref, out_ref, start)


def hidden_of(own_ref, other_ref, low, count):
    width = own_ref.shape[1] // 2
    gates, ups = pl.ds(low, count), pl.ds(width + low, count)
    gate = own_ref[:, gates].astype(F32) + other_ref[:, gates].astype(F32)
    up = own_ref[:, ups].astype(F32) + other_ref[:, ups].astype(F32)
    return (gate / (1.0 + jnp.exp(-gate)) * up).astype(BF16)


def down_first_kernel(count, *refs):
    own, other, (wd_ref, acc_ref) = refs[:count], refs[count : 2 * count], refs[2 * count :]
    total, start = None, 0
    for i in range(count):
        width = own[i].shape[1] // 2
        for low in range(0, width, 512):
            hidden = hidden_of(own[i], other[i], low, 512)
            term = jnp.dot(hidden, wd_ref[pl.ds(start, 512), :], preferred_element_type=F32)
            total = term if total is None else total + term
            start += 512
    acc_ref[...] = total


def down_last_kernel(cap, own_ref, other_ref, wd_ref, acc_ref, *out_refs):
    hidden = hidden_of(own_ref, other_ref, 0, own_ref.shape[1] // 2)
    out = acc_ref[...] + jnp.dot(
        hidden, wd_ref[wd_ref.shape[0] - hidden.shape[1] :, :], preferred_element_type=F32
    )
    half = out.shape[1] // 2
    for o, out_ref in zip(RETURNS, out_refs):
        i = ROWS.index(o)
        out_ref[:cap, :] = out[i * cap : (i + 1) * cap, :half].astype(BF16)
        out_ref[cap:, :] = out[i * cap : (i + 1) * cap, half:].astype(BF16)


def plan_kernel(n, cap, me_ref, ids_ref, weights_ref, pick_ref, scale_ref):
    tok_rows = ids_ref.shape[1]
    rows = slot_rows(ids_ref, me_ref[0], n, cap, tok_rows)
    own = lax.broadcasted_iota(jnp.int32, (tok_rows, tok_rows), 0) == lax.broadcasted_iota(
        jnp.int32, (tok_rows, tok_rows), 1
    )
    number = lax.broadcasted_iota(jnp.int32, (tok_rows, 2 * cap * n), 1)
    for k in range(2):
        weight = jnp.sum(jnp.where(own, weights_ref[k : k + 1, :], 0.0), axis=1, keepdims=True)
        scale_ref[pl.ds(k * tok_rows, tok_rows), :] = jnp.broadcast_to(weight, (tok_rows, 128))
        row = jnp.sum(jnp.where(own, rows[k].astype(F32), 0.0), axis=1, keepdims=True)
        row = row.astype(jnp.int32)
        for part in range(2):
            pick = jnp.where(number == row + part * cap, 1.0, 0.0).astype(BF16)
            pick_ref[pl.ds((2 * part + k) * tok_rows, tok_rows), :] = pick


def combine_kernel(cap, places, pick_ref, scale_ref, *refs):
    n = len(places)
    blocks, (out_hbm, all_ref, out_ref, sems) = refs[:n], refs[n:]
    tok_rows, width = out_ref.shape
    half = width // 2
    for o, block in zip(places, blocks):
        all_ref[pl.ds(o * 2 * cap, 2 * cap), :] = block[...]
    weights = [scale_ref[pl.ds(k * tok_rows, tok_rows), 0:1] for k in range(2)]
    copies = []
    for part in range(2):
        picked = jnp.dot(
            pick_ref[pl.ds(2 * part * tok_rows, 2 * tok_rows), :],
            all_ref[...],
            preferred_element_type=F32,
        )
        total = weights[0] * picked[:tok_rows] + weights[1] * picked[tok_rows:]
        columns = pl.ds(part * half, half)
        out_ref[:, columns] = total.astype(BF16)
        copies.append(
            pltpu.make_async_copy(
                out_ref.at[:, columns], out_hbm.at[:, columns], sems.at[part]
            )
        )
        copies[-1].start()
    for copy in copies:
        copy.wait()


def in_vmem(x):
    return pltpu.with_memory_space_constraint(x, pltpu.VMEM)


def in_hbm(x):
    return pltpu.with_memory_space_constraint(x, pltpu.HBM)


def call(kernel, outs, args, smem=0, hbm=0, scratch=(), limit=20 << 20, cost=None, name=None):
    many = isinstance(outs, (tuple, list))
    result = pl.pallas_call(
        kernel,
        out_shape=[pltpu.VMEM(o.shape, o.dtype) for o in (outs if many else [outs])],
        in_specs=[SMEM_SPEC] * smem
        + [pl.BlockSpec(memory_space=pltpu.HBM)] * hbm
        + [VMEM_SPEC] * (len(args) - smem - hbm),
        out_specs=[VMEM_SPEC] * (len(outs) if many else 1),
        scratch_shapes=scratch,
        compiler_params=pltpu.CompilerParams(vmem_limit_bytes=limit),
        cost_estimate=cost,
        name=name,
    )(*args[: smem + hbm], *(in_vmem(a) for a in args[smem + hbm :]))
    return result if many else result[0]


def swap(x, axis, distance):
    if distance == 0:
        return x
    return lax.ppermute(x, axis, [(i, i ^ distance) for i in range(lax.axis_size(axis))])


def experts(blocks, cap, w_gate, w_up, w_down):
    rows, width = len(blocks) * cap, 2 * blocks[0].shape[1]
    own, other, start = [], [], 0
    for piece in PIECES:
        out = jax.ShapeDtypeStruct((rows, 2 * piece), BF16)
        if start == 0:
            part, x = call(
                lambda *refs: gate_up_first_kernel(cap, *refs),
                [out, jax.ShapeDtypeStruct((rows, width), BF16)],
                [*blocks, w_gate, w_up, w_down],
                cost=estimate(),
                name="gate_up_first",
            )
        else:
            part = call(
                lambda *refs, start=start: gate_up_next_kernel(start, *refs),
                out,
                [x, w_gate, w_up],
                cost=estimate(),
                name="gate_up_next",
            )
        own.append(part)
        other.append(swap(part, "tensor", 1))
        start += piece
    acc = call(
        lambda *refs: down_first_kernel(len(PIECES) - 1, *refs),
        jax.ShapeDtypeStruct((rows, width), F32),
        [*own[:-1], *other[:-1], w_down],
        cost=estimate(),
        name="down_first",
    )
    return call(
        lambda *refs: down_last_kernel(cap, *refs),
        [jax.ShapeDtypeStruct(b.shape, b.dtype) for b in blocks],
        [own[-1], other[-1], w_down, acc],
        cost=estimate(),
        name="down_last",
    )


def estimate():
    return pl.CostEstimate(flops=1, bytes_accessed=0, transcendentals=0)


def one_expert_each(tokens, expert_ids, gate_weights, w_gate, w_up, w_down):
    tok_rows, width = tokens.shape
    n = lax.axis_size("expert")
    cap = capacity_of(tok_rows, expert_ids.shape[1], n)
    half = width // 2
    me = lax.axis_index("expert").astype(jnp.int32).reshape(1)
    ids = expert_ids.T
    loaded = sum(w.size * 2 for w in (w_gate, w_up, w_down))
    block = jax.ShapeDtypeStruct((2 * cap, half), BF16)

    sent = call(
        lambda *refs: dispatch_kernel(n, cap, *refs),
        [block] * n,
        [me, in_hbm(ids), in_hbm(tokens)],
        smem=1,
        hbm=2,
        scratch=[
            pltpu.VMEM(ids.shape, ids.dtype),
            pltpu.VMEM(tokens.shape, tokens.dtype),
            pltpu.SemaphoreType.DMA((2,)),
        ],
        cost=pl.CostEstimate(flops=20_000_000_000, bytes_accessed=2 * loaded, transcendentals=0),
        name="dispatch",
    )
    received = {o: swap(x, "expert", o) for o, x in zip(STARTS, sent)}
    results = experts([received[o] for o in ROWS], cap, w_gate, w_up, w_down)
    returned = {o: swap(x, "expert", o) for o, x in zip(RETURNS, results)}
    pick, scale = call(
        lambda *refs: plan_kernel(n, cap, *refs),
        [
            jax.ShapeDtypeStruct((4 * tok_rows, 2 * cap * n), BF16),
            jax.ShapeDtypeStruct((2 * tok_rows, 128), F32),
        ],
        [me, ids, gate_weights.T],
        smem=1,
        cost=estimate(),
        name="plan",
    )
    return pl.pallas_call(
        lambda *refs: combine_kernel(cap, PLACES, *refs),
        out_shape=jax.ShapeDtypeStruct((tok_rows, width), BF16),
        in_specs=[VMEM_SPEC] * (2 + n),
        out_specs=pl.BlockSpec(memory_space=pl.ANY),
        scratch_shapes=[
            pltpu.VMEM((2 * cap * n, half), BF16),
            pltpu.VMEM((tok_rows, width), BF16),
            pltpu.SemaphoreType.DMA((2,)),
        ],
        compiler_params=pltpu.CompilerParams(vmem_limit_bytes=20 << 20),
        name="combine",
    )(*(in_vmem(x) for x in (pick, scale, *(returned[o] for o in PLACES))))


def per_device(tokens, expert_ids, gate_weights, w_gate, w_up, w_down):
    args = (tokens, expert_ids, gate_weights, w_gate, w_up, w_down)
    whole = w_gate.shape[1] == FF and lax.axis_size("expert") == 8 and lax.axis_size("tensor") == 2
    if whole and expert_ids.shape[1] == 2:
        return one_expert_each(*args)
    return general(*args)


def solution(mesh):
    in_specs = (
        P(("group", "expert"), "tensor"),
        P(("group", "expert"), None),
        P(("group", "expert"), None),
        P("tensor", "expert"),
        P("tensor", "expert"),
        P("expert", "tensor"),
    )
    out_specs = P(("group", "expert"), "tensor")
    return jax.shard_map(
        per_device, mesh=mesh, in_specs=in_specs, out_specs=out_specs, check_vma=False
    )
```

```python
import jax
import jax.numpy as jnp
from jax import lax
from jax.experimental import pallas as pl
from jax.experimental.pallas import tpu as pltpu
from jax.sharding import PartitionSpec as P

FF = 2048
BF16 = jnp.bfloat16
F32 = jnp.float32
VMEM_SPEC = pl.BlockSpec(memory_space=pltpu.VMEM)
SMEM_SPEC = pl.BlockSpec(memory_space=pltpu.SMEM)
PIECES = (2,)
PIECES = (1024, 512, 512)
STARTS = (6, 1, 4, 3, 5, 7, 2, 0)
ROWS = (6, 1, 4, 3, 5, 7, 2, 0)
RETURNS = (6, 1, 4, 3, 5, 7, 2, 0)
PLACES = (6, 1, 4, 3, 5, 7, 2, 0)


def pair_slots(id_blocks, expert_count):
    onehot = (
        id_blocks[:, :, None] == jnp.arange(expert_count, dtype=jnp.int32)[None, None, :]
    ).astype(jnp.int32)
    earlier = jnp.cumsum(onehot, axis=1) - onehot
    return jnp.sum(earlier * onehot, axis=2)


def capacity_of(tok_rows, top_count, expert_count):
    return min(tok_rows, (5 * tok_rows * top_count + 4 * expert_count - 1) // (4 * expert_count))


def general(tokens, expert_ids, gate_weights, w_gate, w_up, w_down):
    tok_rows, half_width = tokens.shape
    top_count = expert_ids.shape[1]
    index_count = lax.axis_size("expert")
    part_width = w_gate.shape[1]
    span_count = FF // part_width
    expert_count = index_count // span_count
    capacity = capacity_of(tok_rows, top_count, expert_count)
    slot_index = pair_slots(expert_ids.reshape(1, tok_rows * top_count), expert_count).reshape(
        tok_rows, top_count
    )
    target = expert_ids * capacity + slot_index
    columns = jnp.arange(expert_count * capacity, dtype=jnp.int32)
    matches = target[:, :, None] == columns[None, None, :]
    selector = jnp.sum(matches.astype(BF16), axis=1)
    weights_table = jnp.sum(jnp.where(matches, gate_weights[:, :, None], 0.0), axis=1)
    buffer = lax.dot_general(
        selector, tokens, (((0,), (0,)), ((), ())), preferred_element_type=F32
    ).astype(BF16)
    buffer = jnp.repeat(buffer.reshape(expert_count, capacity, half_width), span_count, axis=0)
    received = lax.all_to_all(buffer, "expert", split_axis=0, concat_axis=0, tiled=True)
    sources, slot_count, feature_width = received.shape
    flat_rows = received.reshape(sources * slot_count, feature_width)
    gate_part = jnp.dot(flat_rows, w_gate, preferred_element_type=F32).astype(BF16)
    up_part = jnp.dot(flat_rows, w_up, preferred_element_type=F32).astype(BF16)
    gate_full = lax.psum(gate_part, "tensor").astype(F32)
    up_full = lax.psum(up_part, "tensor").astype(F32)
    hidden = (jax.nn.silu(gate_full) * up_full).astype(BF16)
    partial_value = jnp.dot(hidden, w_down, preferred_element_type=F32).astype(BF16)
    results = partial_value.reshape(sources, slot_count, partial_value.shape[1])
    returned = lax.all_to_all(results, "expert", split_axis=0, concat_axis=0, tiled=True)
    by_expert = jnp.sum(
        returned.reshape(expert_count, span_count, capacity, half_width).astype(F32), axis=1
    )
    combined = jnp.dot(
        weights_table,
        by_expert.reshape(expert_count * capacity, half_width),
        precision=lax.Precision.HIGHEST,
        preferred_element_type=F32,
    )
    return combined.astype(BF16)


def slot_rows(ids_ref, me, n, cap, tok_rows):
    shape = (n, tok_rows)
    expert = lax.broadcasted_iota(jnp.int32, shape, 0)
    first = (ids_ref[0:1, :] == expert).astype(F32)
    second = (ids_ref[1:2, :] == expert).astype(F32)
    before = (
        lax.broadcasted_iota(jnp.int32, (tok_rows, tok_rows), 0)
        < lax.broadcasted_iota(jnp.int32, (tok_rows, tok_rows), 1)
    ).astype(BF16)
    earlier = jnp.dot((first + second).astype(BF16), before, preferred_element_type=F32)
    slots = (
        jnp.sum(earlier * first, axis=0, keepdims=True),
        jnp.sum((earlier + first) * second, axis=0, keepdims=True),
    )
    return [
        (ids_ref[k : k + 1, :] ^ me) * (2 * cap) + slots[k].astype(jnp.int32) for k in range(2)
    ]


def dispatch_kernel(n, cap, me_ref, ids_hbm, tok_hbm, *refs):
    out_refs, (ids_ref, tok_ref, sems) = refs[:n], refs[n:]
    tok_rows, half = tok_ref.shape[0] // 2, tok_ref.shape[1]
    ids_copy = pltpu.make_async_copy(ids_hbm, ids_ref, sems.at[0])
    tok_copies = [
        pltpu.make_async_copy(
            tok_hbm.at[:, pl.ds(part * half, half)],
            tok_ref.at[pl.ds(part * tok_rows, tok_rows), :],
            sems.at[1 + part],
        )
        for part in range(2)
    ]
    ids_copy.start()
    for copy in tok_copies:
        copy.start()
    ids_copy.wait()
    rows = slot_rows(ids_ref, me_ref[0], n, cap, tok_rows)
    rows = [jnp.concatenate([row, row + cap], axis=1) for row in rows]
    number = lax.broadcasted_iota(jnp.int32, (2 * cap * n, 2 * tok_rows), 0)
    pick = jnp.where((number == rows[0]) | (number == rows[1]), 1.0, 0.0).astype(BF16)
    for copy in tok_copies:
        copy.wait()
    packed = jnp.dot(pick, tok_ref[...], preferred_element_type=F32)
    for o, out_ref in zip(STARTS, out_refs):
        out_ref[...] = packed[o * 2 * cap : (o + 1) * 2 * cap].astype(BF16)


def gate_up(x_ref, wg_ref, wu_ref, out_ref, start):
    width = out_ref.shape[1] // 2
    tile = 256
    for which, w_ref in enumerate((wg_ref, wu_ref)):
        for j in range(width // tile):
            columns = pl.ds(start + j * tile, tile)
            out_ref[:, pl.ds(which * width + j * tile, tile)] = jnp.dot(
                x_ref[...], w_ref[:, columns], preferred_element_type=F32
            ).astype(BF16)


def gate_up_first_kernel(cap, *refs):
    blocks, (wg_ref, wu_ref, _, out_ref, x_ref) = refs[:-5], refs[-5:]
    half = blocks[0].shape[1]
    for i, block in enumerate(blocks):
        x_ref[pl.ds(i * cap, cap), :half] = block[:cap, :]
        x_ref[pl.ds(i * cap, cap), half:] = block[cap:, :]
    gate_up(x_ref, wg_ref, wu_ref, out_ref, 0)


def gate_up_next_kernel(start, x_ref, wg_ref, wu_ref, out_ref):
    gate_up(x_ref, wg_ref, wu_ref, out_ref, start)


def hidden_of(own_ref, other_ref, low, count):
    width = own_ref.shape[1] // 2
    gates, ups = pl.ds(low, count), pl.ds(width + low, count)
    gate = own_ref[:, gates].astype(F32) + other_ref[:, gates].astype(F32)
    up = own_ref[:, ups].astype(F32) + other_ref[:, ups].astype(F32)
    return (gate / (1.0 + jnp.exp(-gate)) * up).astype(BF16)


def down_first_kernel(count, *refs):
    own, other, (wd_ref, acc_ref) = refs[:count], refs[count : 2 * count], refs[2 * count :]
    total, start = None, 0
    for i in range(count):
        width = own[i].shape[1] // 2
        for low in range(0, width, 512):
            hidden = hidden_of(own[i], other[i], low, 512)
            term = jnp.dot(hidden, wd_ref[pl.ds(start, 512), :], preferred_element_type=F32)
            total = term if total is None else total + term
            start += 512
    acc_ref[...] = total


def down_last_kernel(cap, own_ref, other_ref, wd_ref, acc_ref, *out_refs):
    hidden = hidden_of(own_ref, other_ref, 0, own_ref.shape[1] // 2)
    out = acc_ref[...] + jnp.dot(
        hidden, wd_ref[wd_ref.shape[0] - hidden.shape[1] :, :], preferred_element_type=F32
    )
    half = out.shape[1] // 2
    for o, out_ref in zip(RETURNS, out_refs):
        i = ROWS.index(o)
        out_ref[:cap, :] = out[i * cap : (i + 1) * cap, :half].astype(BF16)
        out_ref[cap:, :] = out[i * cap : (i + 1) * cap, half:].astype(BF16)


def plan_kernel(n, cap, me_ref, ids_ref, weights_ref, pick_ref, scale_ref):
    tok_rows = ids_ref.shape[1]
    rows = slot_rows(ids_ref, me_ref[0], n, cap, tok_rows)
    own = lax.broadcasted_iota(jnp.int32, (tok_rows, tok_rows), 0) == lax.broadcasted_iota(
        jnp.int32, (tok_rows, tok_rows), 1
    )
    number = lax.broadcasted_iota(jnp.int32, (tok_rows, 2 * cap * n), 1)
    for k in range(2):
        weight = jnp.sum(jnp.where(own, weights_ref[k : k + 1, :], 0.0), axis=1, keepdims=True)
        scale_ref[pl.ds(k * tok_rows, tok_rows), :] = jnp.broadcast_to(weight, (tok_rows, 128))
        row = jnp.sum(jnp.where(own, rows[k].astype(F32), 0.0), axis=1, keepdims=True)
        row = row.astype(jnp.int32)
        for part in range(2):
            pick = jnp.where(number == row + part * cap, 1.0, 0.0).astype(BF16)
            pick_ref[pl.ds((2 * part + k) * tok_rows, tok_rows), :] = pick


def combine_kernel(cap, places, pick_ref, scale_ref, *refs):
    n = len(places)
    blocks, (out_hbm, all_ref, out_ref, sems) = refs[:n], refs[n:]
    tok_rows, width = out_ref.shape
    half = width // 2
    for o, block in zip(places, blocks):
        all_ref[pl.ds(o * 2 * cap, 2 * cap), :] = block[...]
    weights = [scale_ref[pl.ds(k * tok_rows, tok_rows), 0:1] for k in range(2)]
    copies = []
    for part in range(2):
        picked = jnp.dot(
            pick_ref[pl.ds(2 * part * tok_rows, 2 * tok_rows), :],
            all_ref[...],
            preferred_element_type=F32,
        )
        total = weights[0] * picked[:tok_rows] + weights[1] * picked[tok_rows:]
        columns = pl.ds(part * half, half)
        out_ref[:, columns] = total.astype(BF16)
        copies.append(
            pltpu.make_async_copy(
                out_ref.at[:, columns], out_hbm.at[:, columns], sems.at[part]
            )
        )
        copies[-1].start()
    for copy in copies:
        copy.wait()


def in_vmem(x):
    return pltpu.with_memory_space_constraint(x, pltpu.VMEM)


def in_hbm(x):
    return pltpu.with_memory_space_constraint(x, pltpu.HBM)


def call(kernel, outs, args, smem=0, hbm=0, scratch=(), limit=20 << 20, cost=None, name=None):
    many = isinstance(outs, (tuple, list))
    result = pl.pallas_call(
        kernel,
        out_shape=[pltpu.VMEM(o.shape, o.dtype) for o in (outs if many else [outs])],
        in_specs=[SMEM_SPEC] * smem
        + [pl.BlockSpec(memory_space=pltpu.HBM)] * hbm
        + [VMEM_SPEC] * (len(args) - smem - hbm),
        out_specs=[VMEM_SPEC] * (len(outs) if many else 1),
        scratch_shapes=scratch,
        compiler_params=pltpu.CompilerParams(vmem_limit_bytes=limit),
        cost_estimate=cost,
        name=name,
    )(*args[: smem + hbm], *(in_vmem(a) for a in args[smem + hbm :]))
    return result if many else result[0]


def swap(x, axis, distance):
    if distance == 0:
        return x
    return lax.ppermute(x, axis, [(i, i ^ distance) for i in range(lax.axis_size(axis))])


def experts(blocks, cap, w_gate, w_up, w_down):
    rows, width = len(blocks) * cap, 2 * blocks[0].shape[1]
    own, other, start = [], [], 0
    for piece in PIECES:
        out = jax.ShapeDtypeStruct((rows, 2 * piece), BF16)
        if start == 0:
            part, x = call(
                lambda *refs: gate_up_first_kernel(cap, *refs),
                [out, jax.ShapeDtypeStruct((rows, width), BF16)],
                [*blocks, w_gate, w_up, w_down],
                cost=estimate(),
                name="gate_up_first",
            )
        else:
            part = call(
                lambda *refs, start=start: gate_up_next_kernel(start, *refs),
                out,
                [x, w_gate, w_up],
                cost=estimate(),
                name="gate_up_next",
            )
        own.append(part)
        other.append(swap(part, "tensor", 1))
        start += piece
    acc = call(
        lambda *refs: down_first_kernel(len(PIECES) - 1, *refs),
        jax.ShapeDtypeStruct((rows, width), F32),
        [*own[:-1], *other[:-1], w_down],
        cost=estimate(),
        name="down_first",
    )
    return call(
        lambda *refs: down_last_kernel(cap, *refs),
        [jax.ShapeDtypeStruct(b.shape, b.dtype) for b in blocks],
        [own[-1], other[-1], w_down, acc],
        cost=estimate(),
        name="down_last",
    )


def estimate():
    return pl.CostEstimate(flops=1, bytes_accessed=0, transcendentals=0)


def one_expert_each(tokens, expert_ids, gate_weights, w_gate, w_up, w_down):
    tok_rows, width = tokens.shape
    n = lax.axis_size("expert")
    cap = capacity_of(tok_rows, expert_ids.shape[1], n)
    half = width // 2
    me = lax.axis_index("expert").astype(jnp.int32).reshape(1)
    ids = expert_ids.T
    loaded = sum(w.size * 2 for w in (w_gate, w_up, w_down))
    block = jax.ShapeDtypeStruct((2 * cap, half), BF16)

    sent = call(
        lambda *refs: dispatch_kernel(n, cap, *refs),
        [block] * n,
        [me, in_hbm(ids), in_hbm(tokens)],
        smem=1,
        hbm=2,
        scratch=[
            pltpu.VMEM(ids.shape, ids.dtype),
            pltpu.VMEM((2 * tok_rows, half), tokens.dtype),
            pltpu.SemaphoreType.DMA((3,)),
        ],
        cost=pl.CostEstimate(flops=20_000_000_000, bytes_accessed=2 * loaded, transcendentals=0),
        name="dispatch",
    )
    received = {o: swap(x, "expert", o) for o, x in zip(STARTS, sent)}
    results = experts([received[o] for o in ROWS], cap, w_gate, w_up, w_down)
    returned = {o: swap(x, "expert", o) for o, x in zip(RETURNS, results)}
    pick, scale = call(
        lambda *refs: plan_kernel(n, cap, *refs),
        [
            jax.ShapeDtypeStruct((4 * tok_rows, 2 * cap * n), BF16),
            jax.ShapeDtypeStruct((2 * tok_rows, 128), F32),
        ],
        [me, ids, gate_weights.T],
        smem=1,
        cost=estimate(),
        name="plan",
    )
    return pl.pallas_call(
        lambda *refs: combine_kernel(cap, PLACES, *refs),
        out_shape=jax.ShapeDtypeStruct((tok_rows, width), BF16),
        in_specs=[VMEM_SPEC] * (2 + n),
        out_specs=pl.BlockSpec(memory_space=pl.ANY),
        scratch_shapes=[
            pltpu.VMEM((2 * cap * n, half), BF16),
            pltpu.VMEM((tok_rows, width), BF16),
            pltpu.SemaphoreType.DMA((2,)),
        ],
        compiler_params=pltpu.CompilerParams(vmem_limit_bytes=20 << 20),
        name="combine",
    )(*(in_vmem(x) for x in (pick, scale, *(returned[o] for o in PLACES))))


def per_device(tokens, expert_ids, gate_weights, w_gate, w_up, w_down):
    args = (tokens, expert_ids, gate_weights, w_gate, w_up, w_down)
    whole = w_gate.shape[1] == FF and lax.axis_size("expert") == 8 and lax.axis_size("tensor") == 2
    if whole and expert_ids.shape[1] == 2:
        return one_expert_each(*args)
    return general(*args)


def solution(mesh):
    in_specs = (
        P(("group", "expert"), "tensor"),
        P(("group", "expert"), None),
        P(("group", "expert"), None),
        P("tensor", "expert"),
        P("tensor", "expert"),
        P("expert", "tensor"),
    )
    out_specs = P(("group", "expert"), "tensor")
    return jax.shard_map(
        per_device, mesh=mesh, in_specs=in_specs, out_specs=out_specs, check_vma=False
    )
```

```python
import jax
import jax.numpy as jnp
from jax import lax
from jax.experimental import pallas as pl
from jax.experimental.pallas import tpu as pltpu
from jax.sharding import PartitionSpec as P

FF = 2048
BF16 = jnp.bfloat16
F32 = jnp.float32
VMEM_SPEC = pl.BlockSpec(memory_space=pltpu.VMEM)
SMEM_SPEC = pl.BlockSpec(memory_space=pltpu.SMEM)
PIECES = (2,)
PIECES = (1024, 512, 512)
STARTS = (6, 1, 4, 3, 5, 7, 2, 0)
ROWS = (6, 1, 4, 3, 5, 7, 2, 0)
RETURNS = (6, 1, 4, 3, 5, 7, 2, 0)
PLACES = (6, 1, 4, 3, 5, 7, 2, 0)


def pair_slots(id_blocks, expert_count):
    onehot = (
        id_blocks[:, :, None] == jnp.arange(expert_count, dtype=jnp.int32)[None, None, :]
    ).astype(jnp.int32)
    earlier = jnp.cumsum(onehot, axis=1) - onehot
    return jnp.sum(earlier * onehot, axis=2)


def capacity_of(tok_rows, top_count, expert_count):
    return min(tok_rows, (5 * tok_rows * top_count + 4 * expert_count - 1) // (4 * expert_count))


def general(tokens, expert_ids, gate_weights, w_gate, w_up, w_down):
    tok_rows, half_width = tokens.shape
    top_count = expert_ids.shape[1]
    index_count = lax.axis_size("expert")
    part_width = w_gate.shape[1]
    span_count = FF // part_width
    expert_count = index_count // span_count
    capacity = capacity_of(tok_rows, top_count, expert_count)
    slot_index = pair_slots(expert_ids.reshape(1, tok_rows * top_count), expert_count).reshape(
        tok_rows, top_count
    )
    target = expert_ids * capacity + slot_index
    columns = jnp.arange(expert_count * capacity, dtype=jnp.int32)
    matches = target[:, :, None] == columns[None, None, :]
    selector = jnp.sum(matches.astype(BF16), axis=1)
    weights_table = jnp.sum(jnp.where(matches, gate_weights[:, :, None], 0.0), axis=1)
    buffer = lax.dot_general(
        selector, tokens, (((0,), (0,)), ((), ())), preferred_element_type=F32
    ).astype(BF16)
    buffer = jnp.repeat(buffer.reshape(expert_count, capacity, half_width), span_count, axis=0)
    received = lax.all_to_all(buffer, "expert", split_axis=0, concat_axis=0, tiled=True)
    sources, slot_count, feature_width = received.shape
    flat_rows = received.reshape(sources * slot_count, feature_width)
    gate_part = jnp.dot(flat_rows, w_gate, preferred_element_type=F32).astype(BF16)
    up_part = jnp.dot(flat_rows, w_up, preferred_element_type=F32).astype(BF16)
    gate_full = lax.psum(gate_part, "tensor").astype(F32)
    up_full = lax.psum(up_part, "tensor").astype(F32)
    hidden = (jax.nn.silu(gate_full) * up_full).astype(BF16)
    partial_value = jnp.dot(hidden, w_down, preferred_element_type=F32).astype(BF16)
    results = partial_value.reshape(sources, slot_count, partial_value.shape[1])
    returned = lax.all_to_all(results, "expert", split_axis=0, concat_axis=0, tiled=True)
    by_expert = jnp.sum(
        returned.reshape(expert_count, span_count, capacity, half_width).astype(F32), axis=1
    )
    combined = jnp.dot(
        weights_table,
        by_expert.reshape(expert_count * capacity, half_width),
        precision=lax.Precision.HIGHEST,
        preferred_element_type=F32,
    )
    return combined.astype(BF16)


def slot_rows(ids_ref, me, n, cap, tok_rows):
    shape = (n, tok_rows)
    expert = lax.broadcasted_iota(jnp.int32, shape, 0)
    first = (ids_ref[0:1, :] == expert).astype(F32)
    second = (ids_ref[1:2, :] == expert).astype(F32)
    before = (
        lax.broadcasted_iota(jnp.int32, (tok_rows, tok_rows), 0)
        < lax.broadcasted_iota(jnp.int32, (tok_rows, tok_rows), 1)
    ).astype(BF16)
    earlier = jnp.dot((first + second).astype(BF16), before, preferred_element_type=F32)
    slots = (
        jnp.sum(earlier * first, axis=0, keepdims=True),
        jnp.sum((earlier + first) * second, axis=0, keepdims=True),
    )
    return [
        (ids_ref[k : k + 1, :] ^ me) * (2 * cap) + slots[k].astype(jnp.int32) for k in range(2)
    ]


def dispatch_kernel(n, cap, me_ref, ids_hbm, tok_hbm, *refs):
    out_refs, (ids_ref, tok_ref, sems) = refs[:n], refs[n:]
    tok_rows, half = tok_ref.shape[0] // 2, tok_ref.shape[1]
    ids_copy = pltpu.make_async_copy(ids_hbm, ids_ref, sems.at[0])
    tok_copies = [
        pltpu.make_async_copy(
            tok_hbm.at[pl.ds(row, tok_rows // 2), pl.ds(part * half, half)],
            tok_ref.at[pl.ds(part * tok_rows + row, tok_rows // 2), :],
            sems.at[1 + 2 * part + i],
        )
        for part in range(2)
        for i, row in enumerate((0, tok_rows // 2))
    ]
    ids_copy.start()
    for copy in tok_copies:
        copy.start()
    ids_copy.wait()
    rows = slot_rows(ids_ref, me_ref[0], n, cap, tok_rows)
    rows = [jnp.concatenate([row, row + cap], axis=1) for row in rows]
    number = lax.broadcasted_iota(jnp.int32, (2 * cap * n, 2 * tok_rows), 0)
    pick = jnp.where((number == rows[0]) | (number == rows[1]), 1.0, 0.0).astype(BF16)
    for copy in tok_copies:
        copy.wait()
    packed = jnp.dot(pick, tok_ref[...], preferred_element_type=F32)
    for o, out_ref in zip(STARTS, out_refs):
        out_ref[...] = packed[o * 2 * cap : (o + 1) * 2 * cap].astype(BF16)


def gate_up(x_ref, wg_ref, wu_ref, out_ref, start):
    width = out_ref.shape[1] // 2
    tile = 256
    for which, w_ref in enumerate((wg_ref, wu_ref)):
        for j in range(width // tile):
            columns = pl.ds(start + j * tile, tile)
            out_ref[:, pl.ds(which * width + j * tile, tile)] = jnp.dot(
                x_ref[...], w_ref[:, columns], preferred_element_type=F32
            ).astype(BF16)


def gate_up_first_kernel(cap, *refs):
    blocks, (wg_ref, wu_ref, _, out_ref, x_ref) = refs[:-5], refs[-5:]
    half = blocks[0].shape[1]
    for i, block in enumerate(blocks):
        x_ref[pl.ds(i * cap, cap), :half] = block[:cap, :]
        x_ref[pl.ds(i * cap, cap), half:] = block[cap:, :]
    gate_up(x_ref, wg_ref, wu_ref, out_ref, 0)


def gate_up_next_kernel(start, x_ref, wg_ref, wu_ref, out_ref):
    gate_up(x_ref, wg_ref, wu_ref, out_ref, start)


def hidden_of(own_ref, other_ref, low, count):
    width = own_ref.shape[1] // 2
    gates, ups = pl.ds(low, count), pl.ds(width + low, count)
    gate = own_ref[:, gates].astype(F32) + other_ref[:, gates].astype(F32)
    up = own_ref[:, ups].astype(F32) + other_ref[:, ups].astype(F32)
    return (gate / (1.0 + jnp.exp(-gate)) * up).astype(BF16)


def down_first_kernel(count, *refs):
    own, other, (wd_ref, acc_ref) = refs[:count], refs[count : 2 * count], refs[2 * count :]
    total, start = None, 0
    for i in range(count):
        width = own[i].shape[1] // 2
        for low in range(0, width, 256):
            hidden = hidden_of(own[i], other[i], low, 256)
            term = jnp.dot(hidden, wd_ref[pl.ds(start, 256), :], preferred_element_type=F32)
            total = term if total is None else total + term
            start += 256
    acc_ref[...] = total


def down_last_kernel(cap, own_ref, other_ref, wd_ref, acc_ref, *out_refs):
    hidden = hidden_of(own_ref, other_ref, 0, own_ref.shape[1] // 2)
    out = acc_ref[...] + jnp.dot(
        hidden, wd_ref[wd_ref.shape[0] - hidden.shape[1] :, :], preferred_element_type=F32
    )
    half = out.shape[1] // 2
    for o, out_ref in zip(RETURNS, out_refs):
        i = ROWS.index(o)
        out_ref[:cap, :] = out[i * cap : (i + 1) * cap, :half].astype(BF16)
        out_ref[cap:, :] = out[i * cap : (i + 1) * cap, half:].astype(BF16)


def plan_kernel(n, cap, me_ref, ids_ref, weights_ref, pick_ref, scale_ref):
    tok_rows = ids_ref.shape[1]
    rows = slot_rows(ids_ref, me_ref[0], n, cap, tok_rows)
    own = lax.broadcasted_iota(jnp.int32, (tok_rows, tok_rows), 0) == lax.broadcasted_iota(
        jnp.int32, (tok_rows, tok_rows), 1
    )
    number = lax.broadcasted_iota(jnp.int32, (tok_rows, 2 * cap * n), 1)
    for k in range(2):
        weight = jnp.sum(jnp.where(own, weights_ref[k : k + 1, :], 0.0), axis=1, keepdims=True)
        scale_ref[pl.ds(k * tok_rows, tok_rows), :] = jnp.broadcast_to(weight, (tok_rows, 128))
        row = jnp.sum(jnp.where(own, rows[k].astype(F32), 0.0), axis=1, keepdims=True)
        row = row.astype(jnp.int32)
        for part in range(2):
            pick = jnp.where(number == row + part * cap, 1.0, 0.0).astype(BF16)
            pick_ref[pl.ds((2 * part + k) * tok_rows, tok_rows), :] = pick


def combine_kernel(cap, places, pick_ref, scale_ref, *refs):
    n = len(places)
    blocks, (out_hbm, all_ref, out_ref, sems) = refs[:n], refs[n:]
    tok_rows, width = out_ref.shape
    half = width // 2
    for o, block in zip(places, blocks):
        all_ref[pl.ds(o * 2 * cap, 2 * cap), :] = block[...]
    weights = [scale_ref[pl.ds(k * tok_rows, tok_rows), 0:1] for k in range(2)]
    copies = []
    for part in range(2):
        picked = jnp.dot(
            pick_ref[pl.ds(2 * part * tok_rows, 2 * tok_rows), :],
            all_ref[...],
            preferred_element_type=F32,
        )
        total = weights[0] * picked[:tok_rows] + weights[1] * picked[tok_rows:]
        columns = pl.ds(part * half, half)
        out_ref[:, columns] = total.astype(BF16)
        copies.append(
            pltpu.make_async_copy(
                out_ref.at[:, columns], out_hbm.at[:, columns], sems.at[part]
            )
        )
        copies[-1].start()
    for copy in copies:
        copy.wait()


def in_vmem(x):
    return pltpu.with_memory_space_constraint(x, pltpu.VMEM)


def in_hbm(x):
    return pltpu.with_memory_space_constraint(x, pltpu.HBM)


def call(kernel, outs, args, smem=0, hbm=0, scratch=(), limit=20 << 20, cost=None, name=None):
    many = isinstance(outs, (tuple, list))
    result = pl.pallas_call(
        kernel,
        out_shape=[pltpu.VMEM(o.shape, o.dtype) for o in (outs if many else [outs])],
        in_specs=[SMEM_SPEC] * smem
        + [pl.BlockSpec(memory_space=pltpu.HBM)] * hbm
        + [VMEM_SPEC] * (len(args) - smem - hbm),
        out_specs=[VMEM_SPEC] * (len(outs) if many else 1),
        scratch_shapes=scratch,
        compiler_params=pltpu.CompilerParams(vmem_limit_bytes=limit),
        cost_estimate=cost,
        name=name,
    )(*args[: smem + hbm], *(in_vmem(a) for a in args[smem + hbm :]))
    return result if many else result[0]


def swap(x, axis, distance):
    if distance == 0:
        return x
    return lax.ppermute(x, axis, [(i, i ^ distance) for i in range(lax.axis_size(axis))])


def experts(blocks, cap, w_gate, w_up, w_down):
    rows, width = len(blocks) * cap, 2 * blocks[0].shape[1]
    own, other, start = [], [], 0
    for piece in PIECES:
        out = jax.ShapeDtypeStruct((rows, 2 * piece), BF16)
        if start == 0:
            part, x = call(
                lambda *refs: gate_up_first_kernel(cap, *refs),
                [out, jax.ShapeDtypeStruct((rows, width), BF16)],
                [*blocks, w_gate, w_up, w_down],
                cost=estimate(),
                name="gate_up_first",
            )
        else:
            part = call(
                lambda *refs, start=start: gate_up_next_kernel(start, *refs),
                out,
                [x, w_gate, w_up],
                cost=estimate(),
                name="gate_up_next",
            )
        own.append(part)
        other.append(swap(part, "tensor", 1))
        start += piece
    acc = call(
        lambda *refs: down_first_kernel(len(PIECES) - 1, *refs),
        jax.ShapeDtypeStruct((rows, width), F32),
        [*own[:-1], *other[:-1], w_down],
        cost=estimate(),
        name="down_first",
    )
    return call(
        lambda *refs: down_last_kernel(cap, *refs),
        [jax.ShapeDtypeStruct(b.shape, b.dtype) for b in blocks],
        [own[-1], other[-1], w_down, acc],
        cost=estimate(),
        name="down_last",
    )


def estimate():
    return pl.CostEstimate(flops=1, bytes_accessed=0, transcendentals=0)


def one_expert_each(tokens, expert_ids, gate_weights, w_gate, w_up, w_down):
    tok_rows, width = tokens.shape
    n = lax.axis_size("expert")
    cap = capacity_of(tok_rows, expert_ids.shape[1], n)
    half = width // 2
    me = lax.axis_index("expert").astype(jnp.int32).reshape(1)
    ids = expert_ids.T
    loaded = sum(w.size * 2 for w in (w_gate, w_up, w_down))
    block = jax.ShapeDtypeStruct((2 * cap, half), BF16)

    sent = call(
        lambda *refs: dispatch_kernel(n, cap, *refs),
        [block] * n,
        [me, in_hbm(ids), in_hbm(tokens)],
        smem=1,
        hbm=2,
        scratch=[
            pltpu.VMEM(ids.shape, ids.dtype),
            pltpu.VMEM((2 * tok_rows, half), tokens.dtype),
            pltpu.SemaphoreType.DMA((5,)),
        ],
        cost=pl.CostEstimate(flops=20_000_000_000, bytes_accessed=2 * loaded, transcendentals=0),
        name="dispatch",
    )
    received = {o: swap(x, "expert", o) for o, x in zip(STARTS, sent)}
    results = experts([received[o] for o in ROWS], cap, w_gate, w_up, w_down)
    returned = {o: swap(x, "expert", o) for o, x in zip(RETURNS, results)}
    pick, scale = call(
        lambda *refs: plan_kernel(n, cap, *refs),
        [
            jax.ShapeDtypeStruct((4 * tok_rows, 2 * cap * n), BF16),
            jax.ShapeDtypeStruct((2 * tok_rows, 128), F32),
        ],
        [me, ids, gate_weights.T],
        smem=1,
        cost=estimate(),
        name="plan",
    )
    return pl.pallas_call(
        lambda *refs: combine_kernel(cap, PLACES, *refs),
        out_shape=jax.ShapeDtypeStruct((tok_rows, width), BF16),
        in_specs=[VMEM_SPEC] * (2 + n),
        out_specs=pl.BlockSpec(memory_space=pl.ANY),
        scratch_shapes=[
            pltpu.VMEM((2 * cap * n, half), BF16),
            pltpu.VMEM((tok_rows, width), BF16),
            pltpu.SemaphoreType.DMA((2,)),
        ],
        compiler_params=pltpu.CompilerParams(vmem_limit_bytes=20 << 20),
        name="combine",
    )(*(in_vmem(x) for x in (pick, scale, *(returned[o] for o in PLACES))))


def per_device(tokens, expert_ids, gate_weights, w_gate, w_up, w_down):
    args = (tokens, expert_ids, gate_weights, w_gate, w_up, w_down)
    whole = w_gate.shape[1] == FF and lax.axis_size("expert") == 8 and lax.axis_size("tensor") == 2
    if whole and expert_ids.shape[1] == 2:
        return one_expert_each(*args)
    return general(*args)


def solution(mesh):
    in_specs = (
        P(("group", "expert"), "tensor"),
        P(("group", "expert"), None),
        P(("group", "expert"), None),
        P("tensor", "expert"),
        P("tensor", "expert"),
        P("expert", "tensor"),
    )
    out_specs = P(("group", "expert"), "tensor")
    return jax.shard_map(
        per_device, mesh=mesh, in_specs=in_specs, out_specs=out_specs, check_vma=False
    )
```
